256 devices in a mesh: lat: 8 (over x_hi, y), lon: 32 (over z, x_lo, core).
Axes of the slice: x: 4 (x_hi: 2, x_lo: 2; x = x_hi * 2 + x_lo), y: 4, z: 8, core: 2. Of those that a mesh axis runs over, the one named last changes fastest.
Arguments:
- fields: bfloat16 [4, 192, 384, 192], P(None, 'lat', 'lon'), may hold values from -43 to 43, as said below
- out_grad: bfloat16 [4, 192, 384, 192], P(None, 'lat', 'lon'), may hold values from -6 to 6
- gain: float32 [192], replicated, may hold values from 0.5 to 1.5
- qkv_weight: bfloat16 [192, 576], replicated, may hold values from -0.4375 to 0.4375
- out_weight: bfloat16 [192, 192], replicated, may hold values from -0.4375 to 0.4375
- window_bias: float32 [16, 2, 6, 20736], P('lat'), may hold values from -4 to 454
Outputs:
- input_grad: bfloat16 [4, 192, 384, 192], P(None, 'lat', 'lon')
- qkv_weight_grad: float32 [192, 576], replicated
- out_weight_grad: float32 [192, 192], replicated
- gain_grad: float32 [192], replicated
- bias_grad: float32 [16, 2, 6, 20736], P('lat')
The draws below stay inside these ranges and needn't reach their ends.
Inputs may be any that keep to these rules, and one draw needn't show every extreme that they name: `fields`: cells have a scale of their own and features a scale of their own.
All inputs are finite; a program needn't handle non-finite values.
Results may differ from the reference program's by a relative error of at most 0.0097.
Values may be sent and summed in bfloat16 or wider, within the bound.
A program may use at most 128 MiB of HBM per device.

```python
import math
import jax
import jax.numpy as jnp
from jax import lax

WIDTH = 192
HEADS = 6
LEVELS = 4
WIN_LEVELS = 2
WIN_LAT = 12
WIN_LON = 6
WIN_TOKENS = 144
LEVEL_WINDOWS = 2
LAT_CELLS = 192
LON_CELLS = 384
LAT_WINDOWS = 16


def draw_fields(key, part):
    key = jax.random.fold_in(key, 11)
    key_channel, key_cell, key_base = jax.random.split(key, 3)
    shape = (LEVELS, LAT_CELLS, LON_CELLS, WIDTH)
    channel = jnp.exp(jax.random.uniform(key_channel, (WIDTH,), minval=math.log(0.3), maxval=math.log(3.0)))
    cell = jnp.exp(jax.random.uniform(key_cell, (LEVELS, LAT_CELLS, LON_CELLS, 1), minval=math.log(0.3), maxval=math.log(3.0)))
    result = jnp.clip(jax.random.normal(key_base, shape), -4.0, 4.0) * channel * cell
    return result.astype(jnp.bfloat16)


def draw_window_bias(key, part):
    key = jax.random.fold_in(key, 23)
    keys = jax.random.split(key, 1)
    shape = (LAT_WINDOWS, LEVEL_WINDOWS, HEADS, WIN_TOKENS, WIN_TOKENS)
    result = jnp.clip(jax.random.normal(keys[0], shape), -4.0, 4.0)
    result = result.reshape(LAT_WINDOWS, LEVEL_WINDOWS, HEADS, WIN_TOKENS * WIN_TOKENS)
    return result.astype(jnp.float32)


def steps_of(own_key, shape, shards, least, largest):
    def one(dim, parts):
        draws = jax.random.uniform(jax.random.fold_in(jax.random.fold_in(own_key, 6), dim), (parts,), jnp.float32, least / len(shards), largest / len(shards))
        return jnp.repeat(jnp.exp(draws), shape[dim] // parts).reshape((-1,) + (1,) * (len(shape) - dim - 1))

    loudness = one(*shards[0])
    for cut in shards[1:]:
        loudness = loudness * one(*cut)
    return loudness


def noise(key, dims, deviation, bound, shards=(), held_as=jnp.bfloat16):
    level = steps_of(key, dims, shards, -0.22, 0.18) if shards else 1.0
    array = jax.random.normal(key, dims, jnp.float32) * deviation * level
    return jnp.minimum(jnp.maximum(array, -bound), bound).astype(held_as)


def setup_inputs(seed: int = 0) -> dict:
    splits = jax.random.split(jax.random.key(seed), 7)
    fields = draw_fields(jax.random.fold_in(splits[6], 71), 0)
    out_grad = noise(splits[1], (LEVELS, LAT_CELLS, LON_CELLS, WIDTH), 1.0, 6.0, ((1, 8), (2, 32)))
    gain = jnp.clip(1.0 + 0.1 * jax.random.normal(splits[2], (WIDTH,), jnp.float32), 0.5, 1.5)
    qkv_weight = noise(splits[3], (WIDTH, 3 * WIDTH), WIDTH ** -0.5, 0.4375)
    out_weight = noise(splits[4], (WIDTH, WIDTH), WIDTH ** -0.5, 0.4375)
    window_bias = draw_window_bias(jax.random.fold_in(splits[6], 71), 0)
    return {"fields": fields, "out_grad": out_grad, "gain": gain, "qkv_weight": qkv_weight, "out_weight": out_weight, "window_bias": window_bias}


EPS = 1e-05
MASKED = -1e+30

def to_windows(field, level_windows, lon_windows):
    levels, lat_rows, lon_cols, features = field.shape
    field = field.reshape(level_windows, levels // level_windows, lat_rows, lon_windows, lon_cols // lon_windows, features)
    field = field.transpose(0, 3, 1, 2, 4, 5)
    return field.reshape(-1, features)

def from_windows(flat, levels, lat_rows, lon_cols, level_windows, lon_windows):
    features = flat.shape[1]
    field = flat.reshape(level_windows, lon_windows, levels // level_windows, lat_rows, lon_cols // lon_windows, features)
    field = field.transpose(0, 2, 3, 1, 4, 5)
    return field.reshape(levels, lat_rows, lon_cols, features)

def window_row(normed_row, grad_row, bias_row, lat_group, qkv_weight, out_weight):
    levels, lat_rows, lon_cols, features = normed_row.shape
    level_windows = levels // WIN_LEVELS
    lon_windows = lon_cols // WIN_LON
    head_count = bias_row.shape[1]
    head_width = features // head_count
    score_scale = head_width ** (-0.5)
    position = jnp.arange(WIN_TOKENS)
    level_pos = position // (lat_rows * WIN_LON)
    lat_pos = position // WIN_LON % lat_rows
    token_group = lax.optimization_barrier(jnp.sum(jnp.where(lat_pos[:, None] == jnp.arange(lat_rows)[None, :], lat_group[None, :], 0), axis=1))
    level_flag = jnp.arange(level_windows)[:, None] * WIN_LEVELS + level_pos[None, :] == levels - 1
    allowed = (token_group[None, :, None] >= 0) & (token_group[None, :, None] == token_group[None, None, :]) & (level_flag[:, :, None] == level_flag[:, None, :])
    inputs = to_windows(normed_row, level_windows, lon_windows)
    upstream = to_windows(grad_row, level_windows, lon_windows)
    live = jnp.broadcast_to(token_group >= 0, (level_windows, lon_windows, WIN_TOKENS)).reshape(-1, 1)
    upstream = jnp.where(live, upstream, jnp.zeros_like(upstream))
    projected = jnp.dot(inputs, qkv_weight, preferred_element_type=jnp.float32)

    def split_heads(block):
        return block.astype(jnp.bfloat16).reshape(level_windows, lon_windows, WIN_TOKENS, head_count, head_width)
    query_heads = split_heads(projected[:, :features])
    key_heads = split_heads(projected[:, features:2 * features])
    value_heads = split_heads(projected[:, 2 * features:])
    f32 = jnp.float32
    scores = jnp.einsum('znqhd,znkhd->znhqk', query_heads.astype(f32), key_heads.astype(f32)) * score_scale + bias_row[:, None]
    scores = jnp.where(allowed[:, None, None], scores, MASKED)
    row_max = lax.optimization_barrier(jnp.max(scores, axis=-1, keepdims=True))
    exps = jnp.exp(scores - row_max)
    attention = exps / lax.optimization_barrier(jnp.sum(exps, axis=-1, keepdims=True))
    attention_low = attention.astype(jnp.bfloat16)
    attended = jnp.einsum('znhqk,znkhd->znqhd', attention_low.astype(f32), value_heads.astype(f32)).astype(jnp.bfloat16).reshape(-1, features)
    out_part = jnp.dot(attended.T, upstream, preferred_element_type=jnp.float32)
    grad_attended = jnp.dot(upstream, out_weight.T, preferred_element_type=jnp.float32).astype(jnp.bfloat16)
    grad_attended = grad_attended.reshape(level_windows, lon_windows, WIN_TOKENS, head_count, head_width)
    grad_attention = jnp.einsum('znqhd,znkhd->znhqk', grad_attended.astype(f32), value_heads.astype(f32))
    grad_values = jnp.einsum('znhqk,znqhd->znkhd', attention_low.astype(f32), grad_attended.astype(f32)).astype(jnp.bfloat16)
    grad_scores = attention * (grad_attention - lax.optimization_barrier(jnp.sum(attention * grad_attention, axis=-1, keepdims=True)))
    bias_part = lax.optimization_barrier(jnp.sum(grad_scores, axis=1))
    grad_scores_low = grad_scores.astype(jnp.bfloat16).astype(f32)
    grad_queries = (jnp.einsum('znhqk,znkhd->znqhd', grad_scores_low, key_heads.astype(f32)) * score_scale).astype(jnp.bfloat16)
    grad_keys = (jnp.einsum('znhqk,znqhd->znkhd', grad_scores_low, query_heads.astype(f32)) * score_scale).astype(jnp.bfloat16)
    grad_projected = jnp.concatenate([grad_queries.reshape(-1, features), grad_keys.reshape(-1, features), grad_values.reshape(-1, features)], axis=1)
    qkv_part = jnp.dot(inputs.T, grad_projected, preferred_element_type=jnp.float32)
    grad_inputs = jnp.dot(grad_projected, qkv_weight.T, preferred_element_type=jnp.float32).astype(jnp.bfloat16)
    grad_inputs = from_windows(grad_inputs, levels, lat_rows, lon_cols, level_windows, lon_windows)
    return (grad_inputs, qkv_part, out_part, bias_part)

def reference(fields, out_grad, gain, qkv_weight, out_weight, window_bias):
    half_lat = WIN_LAT // 2
    half_lon = WIN_LON // 2
    tables = window_bias.reshape(LAT_WINDOWS, LEVEL_WINDOWS, HEADS, WIN_TOKENS, WIN_TOKENS)
    values32 = fields.astype(jnp.float32)
    centred = values32 - lax.optimization_barrier(jnp.mean(values32, axis=-1, keepdims=True))
    inv_std = lax.rsqrt(lax.optimization_barrier(jnp.mean(centred * centred, axis=-1, keepdims=True)) + EPS)
    standard = centred * inv_std
    normed = (standard * gain).astype(jnp.bfloat16)

    def shift_frame(field):
        rolled = jnp.roll(field, -1, axis=0)
        padding = jnp.zeros((LEVELS, half_lat, LON_CELLS, WIDTH), field.dtype)
        padded = jnp.concatenate([padding, rolled, padding], axis=1)
        return jnp.roll(padded, -half_lon, axis=2)
    shifted_in = shift_frame(normed)
    shifted_grad = shift_frame(out_grad)
    row_count = LAT_WINDOWS + 1
    padded_rows = jnp.arange(LAT_CELLS + WIN_LAT)
    row_groups = jnp.where((padded_rows >= half_lat) & (padded_rows < LAT_CELLS + half_lat), 0, -1).astype(jnp.int32)
    bias_rows = jnp.concatenate([tables, tables[LAT_WINDOWS - 1:]], axis=0)

    def stack_rows(field):
        return jnp.moveaxis(field.reshape(LEVELS, row_count, WIN_LAT, LON_CELLS, WIDTH), 1, 0)

    def visit(carry, items):
        part_in, part_grad, part_bias, part_group = items
        grad_inputs, qkv_part, out_part, bias_part = window_row(part_in, part_grad, part_bias, part_group, qkv_weight, out_weight)
        return ((carry[0] + qkv_part, carry[1] + out_part), (grad_inputs, bias_part))
    start = (jnp.zeros((WIDTH, 3 * WIDTH), jnp.float32), jnp.zeros((WIDTH, WIDTH), jnp.float32))
    (qkv_sum, out_sum), (grad_rows, bias_rows_grad) = lax.scan(visit, start, (stack_rows(shifted_in), stack_rows(shifted_grad), bias_rows, row_groups.reshape(row_count, WIN_LAT)))
    bias_grad = bias_rows_grad[:LAT_WINDOWS].at[LAT_WINDOWS - 1].add(bias_rows_grad[LAT_WINDOWS])
    bias_grad = bias_grad.reshape(LAT_WINDOWS, LEVEL_WINDOWS, HEADS, WIN_TOKENS * WIN_TOKENS)
    grad_shifted = jnp.moveaxis(grad_rows, 0, 1).reshape(LEVELS, row_count * WIN_LAT, LON_CELLS, WIDTH)
    grad_normed = jnp.roll(grad_shifted, half_lon, axis=2)[:, half_lat:half_lat + LAT_CELLS]
    grad_normed = jnp.roll(grad_normed, 1, axis=0)
    grad32 = grad_normed.astype(jnp.float32)
    gain_grad = lax.optimization_barrier(jnp.sum(grad32 * standard, axis=(0, 1, 2)))
    scaled = grad32 * gain
    input_grad = out_grad.astype(jnp.float32) + inv_std * (scaled - lax.optimization_barrier(jnp.mean(scaled, axis=-1, keepdims=True)) - standard * lax.optimization_barrier(jnp.mean(scaled * standard, axis=-1, keepdims=True)))
    return (input_grad.astype(jnp.bfloat16), qkv_sum, out_sum, gain_grad, bias_grad)
```

```python
import jax
import jax.numpy as jnp
from jax import lax
from jax.experimental import pallas as pl
from jax.experimental.pallas import tpu as pltpu
from jax.sharding import PartitionSpec as P

F32 = jnp.float32
BF16 = jnp.bfloat16
MESH = pl.DeviceIdType.MESH

EPS = 1e-05
MASKED = -1e30

LEVELS = 4
ROWS = 24
COLS = 12
WIDTH = 192
HEADS = 6
HEAD = 32
TOKENS = 144
HALF = 72
LATS = 8
LONS = 32
Z = 8

BIAS_ROWS = 96
WEIGHT_ROWS = 48
SHARD = BIAS_ROWS + WEIGHT_ROWS
BIAS_ALL = LONS * BIAS_ROWS

VMEM_LIMIT = 56 * 1024 * 1024


def vmem_spec():
    return pl.BlockSpec(memory_space=pltpu.VMEM)


def params(**kw):
    return pltpu.CompilerParams(vmem_limit_bytes=VMEM_LIMIT, **kw)


def pack_in_kernel(fields_ref, grad_ref, a_ref, b_ref, tmp_ref):
    for k, ref in enumerate((fields_ref, grad_ref)):
        for r in range(6):
            for lev in range(LEVELS):
                at = r * 48 + lev * 12
                tmp_ref[at : at + 12, :] = ref[lev, 18 + r].astype(F32)
        a_ref[k] = tmp_ref[...].astype(BF16)
    for k, ref in enumerate((fields_ref, grad_ref)):
        for r in range(ROWS):
            for lev in range(LEVELS):
                at = ((r - 18) % ROWS) * 12 + lev * 3
                tmp_ref[at : at + 3, :] = ref[lev, r].astype(F32)[0:3]
        b_ref[k] = tmp_ref[...].astype(BF16)


def pack_in(fields, grad):
    shape = jax.ShapeDtypeStruct((2, 288, WIDTH), BF16)
    return pl.pallas_call(
        pack_in_kernel,
        out_shape=(shape, shape),
        in_specs=[vmem_spec()] * 2,
        out_specs=(vmem_spec(), vmem_spec()),
        scratch_shapes=[pltpu.VMEM((288, WIDTH), F32)],
        compiler_params=params(),
        name="pack_in",
    )(fields, grad)


def halo_kernel(step, a_ref, b_ref, ra_ref, rb_ref, rc_ref, send, recv):
    lat = lax.axis_index("lat")
    lon = lax.axis_index("lon")
    to_lat = (lat + step + LATS) % LATS
    to_lon = (lon - step + LONS) % LONS
    from_lat = (lat - step + LATS) % LATS
    from_lon = (lon + step + LONS) % LONS
    barrier = pltpu.get_barrier_semaphore()
    for there in ((from_lat, lon), (lat, from_lon), (from_lat, from_lon)):
        pl.semaphore_signal(barrier, inc=1, device_id=there, device_id_type=MESH)
    pl.semaphore_wait(barrier, 3)
    plan = (
        (a_ref, ra_ref, (to_lat, lon)),
        (b_ref, rb_ref, (lat, to_lon)),
        (b_ref.at[:, 0:80], rc_ref, (to_lat, to_lon)),
    )
    copies = [
        pltpu.make_async_remote_copy(
            src_ref=source,
            dst_ref=target,
            send_sem=send.at[k],
            recv_sem=recv.at[k],
            device_id=there,
            device_id_type=MESH,
        )
        for k, (source, target, there) in enumerate(plan)
    ]
    for copy in copies:
        copy.start()
    for copy in copies:
        copy.wait()


def halo(step, a, b):
    return pl.pallas_call(
        lambda *refs: halo_kernel(step, *refs),
        out_shape=(
            jax.ShapeDtypeStruct(a.shape, BF16),
            jax.ShapeDtypeStruct(b.shape, BF16),
            jax.ShapeDtypeStruct((b.shape[0], 80, WIDTH), BF16),
        ),
        in_specs=[vmem_spec()] * 2,
        out_specs=(vmem_spec(),) * 3,
        scratch_shapes=[pltpu.SemaphoreType.DMA((3,)), pltpu.SemaphoreType.DMA((3,))],
        compiler_params=params(collective_id=0 if step == 1 else 1, has_side_effects=True),
        name="halo",
    )(a, b)


def assemble_kernel(fields_ref, grad_ref, a_ref, b_ref, c_ref, xw_ref, gw_ref, tmp_ref, b32_ref, c32_ref):
    lat = lax.axis_index("lat")
    for k, (own, out) in enumerate(((fields_ref, xw_ref), (grad_ref, gw_ref))):
        b32_ref[...] = b_ref[k].astype(F32)
        c32_ref[...] = c_ref[k].astype(F32)
        for w in range(2):
            for g in range(3):
                for zl in range(2):
                    lev = (2 * w + zl + 1) % LEVELS
                    for lp in range(12):
                        at = (zl * 12 + lp) * 6
                        row = 12 * g + lp - 6
                        if row >= ROWS:
                            tmp_ref[0, at : at + 6, :] = jnp.zeros((6, WIDTH), F32)
                            tmp_ref[1, at : at + 6, :] = jnp.zeros((6, WIDTH), F32)
                            continue
                        if row < 0:
                            from_a = (row + 6) * 48 + lev * 12
                            tile = a_ref[k, from_a : from_a + 12, :].astype(F32)
                            from_c = (row + 6) * 12 + lev * 3
                            east = c32_ref[from_c : from_c + 3, :]
                            tile = jnp.where(lat == 0, 0.0, tile)
                            east = jnp.where(lat == 0, 0.0, east)
                        else:
                            tile = own[lev, row].astype(F32)
                            from_b = ((row - 18) % ROWS) * 12 + lev * 3
                            east = b32_ref[from_b : from_b + 3, :]
                        tmp_ref[0, at : at + 6, :] = tile[3:9]
                        tmp_ref[1, at : at + 3, :] = tile[9:12]
                        tmp_ref[1, at + 3 : at + 6, :] = east
                out[w, g] = tmp_ref[...].astype(BF16)


def assemble(fields, grad, a, b, c):
    shape = jax.ShapeDtypeStruct((2, 3, 2, TOKENS, WIDTH), BF16)
    return pl.pallas_call(
        assemble_kernel,
        out_shape=(shape, shape),
        in_specs=[vmem_spec()] * 5,
        out_specs=(vmem_spec(), vmem_spec()),
        scratch_shapes=[
            pltpu.VMEM((2, TOKENS, WIDTH), F32),
            pltpu.VMEM((288, WIDTH), F32),
            pltpu.VMEM((80, WIDTH), F32),
        ],
        compiler_params=params(),
        name="assemble",
    )(fields, grad, a, b, c)


def dot(a, b, contract=(1, 0)):
    return lax.dot_general(
        a, b, (((contract[0],), (contract[1],)), ((), ())), preferred_element_type=F32
    )


def window(n, x_ref, g_ref, gain, qkv_ref, qkv_t_ref, out_ref, bias_ref, first, bias_acc, weight_acc, gain_acc, ig_ref):
    scale = HEAD ** (-0.5)
    x = x_ref[n].astype(F32)
    centred = x - jnp.mean(x, axis=-1, keepdims=True)
    inv_std = lax.rsqrt(jnp.mean(centred * centred, axis=-1, keepdims=True) + EPS)
    standard = centred * inv_std
    normed = (standard * gain).astype(BF16)
    upstream = g_ref[n]
    projected = dot(normed, qkv_ref[...]).astype(BF16)
    projected_t = dot(qkv_t_ref[...], normed, (1, 1)).astype(BF16)
    attended_grad = dot(upstream, out_ref[...], (1, 1)).astype(BF16)
    attended_grad_t = dot(out_ref[...], upstream, (1, 1)).astype(BF16)
    lane = lax.broadcasted_iota(jnp.int32, (TOKENS, 128), 1)
    attended_parts, queries_parts, keys_parts, values_parts = [], [], [], []
    for h in range(HEADS):
        lo = 128 * (h // 4)
        width = 128 if h < 4 else 64
        own = (lane[:, :width] // HEAD) == (h % 4)
        queries = jnp.where(own, projected[:, lo : lo + width], jnp.zeros((), BF16))
        keys = projected[:, WIDTH + lo : WIDTH + lo + width]
        values = projected[:, 2 * WIDTH + lo : 2 * WIDTH + lo + width]
        upper = jnp.where(own, attended_grad[:, lo : lo + width], jnp.zeros((), BF16))
        rows = slice(h * HEAD, (h + 1) * HEAD)
        queries_t = projected_t[h * HEAD : (h + 1) * HEAD]
        keys_t = projected_t[WIDTH + h * HEAD : WIDTH + (h + 1) * HEAD]
        values_t = projected_t[2 * WIDTH + h * HEAD : 2 * WIDTH + (h + 1) * HEAD]
        scores = dot(queries, keys, (1, 1)) * scale + bias_ref[h]
        exps = jnp.exp(scores - jnp.max(scores, axis=-1, keepdims=True))
        attention = exps * (1.0 / jnp.sum(exps, axis=-1, keepdims=True))
        low = attention.astype(BF16)
        attention_grad = dot(upper, values, (1, 1))
        delta = jnp.sum(attention * attention_grad, axis=-1, keepdims=True)
        scores_grad = attention * (attention_grad - delta)
        if n == 0:
            @pl.when(first)
            def _():
                bias_acc[h] = scores_grad

            @pl.when(jnp.logical_not(first))
            def _():
                bias_acc[h] += scores_grad
        else:
            bias_acc[h] += scores_grad
        scores_low = scores_grad.astype(BF16)
        attended_parts.append(dot(values_t, low, (1, 1)).astype(BF16))
        values_parts.append(dot(attended_grad_t[rows], low).astype(BF16))
        queries_parts.append((dot(keys_t, scores_low, (1, 1)) * scale).astype(BF16))
        keys_parts.append((dot(queries_t, scores_low) * scale).astype(BF16))
    attended_t = jnp.concatenate(attended_parts, axis=0)
    projected_grad_t = jnp.concatenate(queries_parts + keys_parts + values_parts, axis=0)
    weight_acc[3 * WIDTH :, :] += dot(attended_t, upstream)
    weight_acc[: 3 * WIDTH, :] += dot(projected_grad_t, normed)
    shifted_t = dot(qkv_ref[...], projected_grad_t)
    grad = jnp.transpose(shifted_t).astype(BF16).astype(F32)
    product = grad * standard
    gain_acc[...] += jnp.sum(product, axis=0, keepdims=True)
    scaled = grad * gain
    ig = upstream.astype(F32) + inv_std * (
        scaled
        - jnp.mean(scaled, axis=-1, keepdims=True)
        - standard * jnp.mean(product * gain, axis=-1, keepdims=True)
    )
    ig_ref[n] = ig.astype(BF16)


def compute_kernel(
    x_ref, g_ref, gain_ref, qkv_ref, qkv_t_ref, out_ref, bias_ref,
    ig_ref, packed_ref, masked, bias_acc, weight_acc, gain_acc, flat,
):
    w, g = pl.program_id(0), pl.program_id(1)
    lat = lax.axis_index("lat")

    @pl.when((w == 0) & (g == 0))
    def _():
        weight_acc[...] = jnp.zeros_like(weight_acc)
        gain_acc[...] = jnp.zeros_like(gain_acc)
        flat[BIAS_ALL - 48 :, :] = jnp.zeros((48, 128), F32)

    @pl.when((g < 2) | (lat == LATS - 1))
    def _():
        q = lax.broadcasted_iota(jnp.int32, (TOKENS, TOKENS), 0)
        k = lax.broadcasted_iota(jnp.int32, (TOKENS, TOKENS), 1)
        half = ((q >= HALF) != (k >= HALF)) & (w == 1)
        q_low = ((q // 6) % 12) < 6
        k_low = ((k // 6) % 12) < 6
        top = (q_low | k_low) & (g == 0) & (lat == 0)
        bottom = jnp.logical_not(q_low & k_low) & (g == 2)
        blocked = half | top | bottom
        for h in range(HEADS):
            masked[h] = jnp.where(blocked, MASKED, bias_ref[0, 0, h])
        gain = gain_ref[...]
        for n in range(2):
            window(
                n, x_ref.at[0, 0], g_ref.at[0, 0], gain, qkv_ref, qkv_t_ref, out_ref, masked, g < 2,
                bias_acc, weight_acc, gain_acc, ig_ref.at[0, 0],
            )

    def fold(at, rows, take):
        tails = []
        for h in range(HEADS):
            value = take(h)
            flat[pl.ds(at + h * rows, rows), :] = value[:, :128]
            tails.append(value[:, 128:])
        tails.append(jnp.zeros((rows, 32), F32))
        flat[pl.ds(at + HEADS * rows, rows), :] = jnp.concatenate(tails, axis=1)

    for which in range(2):
        @pl.when((g == (0, 2)[which]) & (w == 0))
        def _():
            fold(which * 1512, TOKENS, lambda h: bias_acc[h])

        @pl.when((g == (0, 2)[which]) & (w == 1))
        def _():
            fold(which * 1512 + 1008, HALF, lambda h: bias_acc[h, :HALF, :] + bias_acc[h, HALF:, :])

    @pl.when((w == 1) & (g == 2))
    def _():
        zero = jnp.zeros((WEIGHT_ROWS, 128), BF16)
        for s in range(LONS):
            packed_ref[s, :BIAS_ROWS, :] = flat[s * BIAS_ROWS : (s + 1) * BIAS_ROWS, :].astype(BF16)
        for s in range(16):
            packed_ref[s, BIAS_ROWS:, :] = weight_acc[s * 48 : (s + 1) * 48, :128].astype(BF16)
        for s in range(8):
            pair = jnp.concatenate(
                [weight_acc[s * 48 : (s + 1) * 48, 128:], weight_acc[384 + s * 48 : 384 + (s + 1) * 48, 128:]],
                axis=1,
            )
            packed_ref[16 + s, BIAS_ROWS:, :] = pair.astype(BF16)
        total = gain_acc[...]
        left = jnp.broadcast_to(total[:, :128], (WEIGHT_ROWS, 128))
        right = jnp.concatenate([total[:, 128:], jnp.zeros((1, 64), F32)], axis=1)
        right = jnp.broadcast_to(right, (WEIGHT_ROWS, 128))
        row = lax.broadcasted_iota(jnp.int32, (WEIGHT_ROWS, 128), 0)
        packed_ref[24, BIAS_ROWS:, :] = jnp.where(row == 0, left, jnp.where(row == 1, right, 0.0)).astype(BF16)
        for s in range(25, LONS):
            packed_ref[s, BIAS_ROWS:, :] = zero


def compute(xw, gw, gain, qkv, out_weight, bias):
    whole = lambda *shape: pl.BlockSpec(shape, lambda w, g: (0,) * len(shape))
    window_spec = pl.BlockSpec((1, 1, 2, TOKENS, WIDTH), lambda w, g: (w, g, 0, 0, 0))
    return pl.pallas_call(
        compute_kernel,
        grid=(2, 3),
        out_shape=(
            jax.ShapeDtypeStruct((2, 3, 2, TOKENS, WIDTH), BF16),
            jax.ShapeDtypeStruct((LONS, SHARD, 128), BF16),
        ),
        in_specs=[
            window_spec,
            window_spec,
            whole(1, WIDTH),
            whole(WIDTH, 3 * WIDTH),
            whole(3 * WIDTH, WIDTH),
            whole(WIDTH, WIDTH),
            pl.BlockSpec((1, 1, HEADS, TOKENS, TOKENS), lambda w, g: (jnp.minimum(g, 1), w, 0, 0, 0)),
        ],
        out_specs=(window_spec, whole(LONS, SHARD, 128)),
        scratch_shapes=[
            pltpu.VMEM((HEADS, TOKENS, TOKENS), F32),
            pltpu.VMEM((HEADS, TOKENS, TOKENS), F32),
            pltpu.VMEM((4 * WIDTH, WIDTH), F32),
            pltpu.VMEM((1, WIDTH), F32),
            pltpu.VMEM((BIAS_ALL, 128), F32),
        ],
        compiler_params=params(),
        name="windows",
    )(xw, gw, gain.reshape(1, WIDTH), qkv, qkv.T, out_weight, bias)


def pack_out_kernel(ig_ref, tile_ref, e_ref, d_ref, w32_ref, tmp_ref):
    for w in range(2):
        for g in range(3):
            w32_ref[...] = ig_ref[w, g].astype(F32)
            for zl in range(2):
                lev = (2 * w + zl + 1) % LEVELS
                for lp in range(12 if g < 2 else 6):
                    at = (zl * 12 + lp) * 6
                    row = 12 * g + lp - 6
                    tile_ref[lev, row + 6, 3:9, :] = w32_ref[0, at : at + 6, :]
                    tile_ref[lev, row + 6, 9:12, :] = w32_ref[1, at : at + 3, :]
                    tile_ref[lev, row + 6, 0:3, :] = w32_ref[1, at + 3 : at + 6, :]
    for r in range(6):
        for lev in range(LEVELS):
            tmp_ref[r * 48 + lev * 12 : r * 48 + lev * 12 + 12, :] = tile_ref[lev, r]
    e_ref[0] = tmp_ref[:288, :].astype(BF16)
    for r in range(30):
        for lev in range(LEVELS):
            at = r * 12 + lev * 3
            tmp_ref[at : at + 3, :] = tile_ref[lev, r, 0:3, :]
    tmp_ref[360:, :] = jnp.zeros((8, WIDTH), F32)
    d_ref[0] = tmp_ref[...].astype(BF16)


def pack_out(ig):
    return pl.pallas_call(
        pack_out_kernel,
        out_shape=(
            jax.ShapeDtypeStruct((LEVELS, 30, COLS, WIDTH), F32),
            jax.ShapeDtypeStruct((1, 288, WIDTH), BF16),
            jax.ShapeDtypeStruct((1, 368, WIDTH), BF16),
        ),
        in_specs=[vmem_spec()],
        out_specs=(vmem_spec(),) * 3,
        scratch_shapes=[pltpu.VMEM((2, TOKENS, WIDTH), F32), pltpu.VMEM((368, WIDTH), F32)],
        compiler_params=params(),
        name="pack_out",
    )(ig)


def place_kernel(tile_ref, e_ref, d_ref, f_ref, out_ref, d32_ref, f32_ref):
    last = lax.axis_index("lat") == LATS - 1
    d32_ref[...] = d_ref[0].astype(F32)
    f32_ref[...] = f_ref[0].astype(F32)
    column = lax.broadcasted_iota(jnp.int32, (COLS, WIDTH), 0)
    for lev in range(LEVELS):
        for row in range(ROWS):
            if row < 18:
                own = tile_ref[lev, row + 6]
                at = (row + 6) * 12 + lev * 3
                west = d32_ref[at : at + 3, :]
            else:
                r = row - 18
                at = r * 48 + lev * 12
                own = jnp.where(last, tile_ref[lev, 24 + r], e_ref[0, at : at + 12, :].astype(F32))
                at = r * 12 + lev * 3
                west = jnp.where(last, d32_ref[288 + at : 288 + at + 3, :], f32_ref[at : at + 3, :])
            west = jnp.concatenate([west, jnp.zeros((COLS - 3, WIDTH), F32)], axis=0)
            out_ref[lev, row] = jnp.where(column < 3, west, own).astype(BF16)


def place(tiles, e, d, f):
    return pl.pallas_call(
        place_kernel,
        out_shape=jax.ShapeDtypeStruct((LEVELS, ROWS, COLS, WIDTH), BF16),
        in_specs=[vmem_spec()] * 4,
        out_specs=vmem_spec(),
        scratch_shapes=[pltpu.VMEM((368, WIDTH), F32), pltpu.VMEM((80, WIDTH), F32)],
        compiler_params=params(),
        name="place",
    )(tiles, e, d, f)


def sums_kernel(
    src, out, core_buf, x_buf, z_buf, lat_buf, held, weights,
    core_send, core_recv, x_send, x_recv, z_send, z_recv, lat_send, lat_recv,
    gz_send, gz_recv, gw_send, gw_recv, gx_send, gx_recv, gc_send, gc_recv,
):
    lat = lax.axis_index("lat")
    lon = lax.axis_index("lon")
    z, x, core = lon // 4, (lon // 2) % 2, lon % 2

    def at_lon(zz, xx, cc):
        return (lat, zz * 4 + xx * 2 + cc)

    core_peer = at_lon(z, x, 1 - core)
    x_peer = at_lon(z, 1 - x, core)
    z_peers = [at_lon((z + d) % Z, x, core) for d in range(1, Z)]
    lat_peers = [((lat + d) % LATS, lon) for d in range(1, LATS)]
    barrier = pltpu.get_barrier_semaphore()
    for there in [core_peer, x_peer] + z_peers + lat_peers:
        pl.semaphore_signal(barrier, inc=1, device_id=there, device_id_type=MESH)
    pl.semaphore_wait(barrier, 2 + 2 * (Z - 1))

    def copy(source, target, send, recv, there):
        return pltpu.make_async_remote_copy(
            src_ref=source, dst_ref=target, send_sem=send, recv_sem=recv,
            device_id=there, device_id_type=MESH,
        )

    first = copy(src.at[pl.ds((1 - core) * 16, 16)], core_buf, core_send, core_recv, core_peer)
    first.start()
    first.wait()

    @pl.loop(0, 16)
    def _(s):
        held[s] = (src[core * 16 + s].astype(F32) + core_buf[s].astype(F32)).astype(BF16)

    second = copy(held.at[pl.ds((1 - x) * 8, 8)], x_buf, x_send, x_recv, x_peer)
    second.start()
    second.wait()

    @pl.loop(0, 8)
    def _(s):
        x_buf[s] = (held[x * 8 + s].astype(F32) + x_buf[s].astype(F32)).astype(BF16)

    third = [
        copy(x_buf.at[(z + d) % Z], z_buf.at[d - 1], z_send.at[d - 1], z_recv.at[d - 1], z_peers[d - 1])
        for d in range(1, Z)
    ]
    for c in third:
        c.start()
    for c in third:
        c.wait()
    total = x_buf[z].astype(F32)
    for d in range(Z - 1):
        total = total + z_buf[d].astype(F32)
    mine = core * 16 + x * 8 + z
    weights[...] = total[BIAS_ROWS:].astype(BF16)
    lat_buf[lat] = total[BIAS_ROWS:].astype(BF16)
    fourth = [
        copy(weights, lat_buf.at[lat], lat_send.at[d - 1], lat_recv.at[d - 1], lat_peers[d - 1])
        for d in range(1, LATS)
    ]
    for c in fourth:
        c.start()
    out[mine, :BIAS_ROWS, :] = total[:BIAS_ROWS].astype(BF16)
    part = out.at[mine, pl.ds(0, BIAS_ROWS)]
    gather = [
        copy(part, part, gz_send.at[d - 1], gz_recv.at[d - 1], z_peers[d - 1]) for d in range(1, Z)
    ]
    for c in gather:
        c.start()
    for c in fourth:
        c.wait()
    total = lat_buf[0].astype(F32)
    for i in range(1, LATS):
        total = total + lat_buf[i].astype(F32)
    out[mine, BIAS_ROWS:, :] = total.astype(BF16)
    part = out.at[mine, pl.ds(BIAS_ROWS, WEIGHT_ROWS)]
    gather_weights = [
        copy(part, part, gw_send.at[d - 1], gw_recv.at[d - 1], z_peers[d - 1]) for d in range(1, Z)
    ]
    for c in gather_weights:
        c.start()
    for c in gather + gather_weights:
        c.wait()
    part = out.at[pl.ds(core * 16 + x * 8, 8)]
    c = copy(part, part, gx_send, gx_recv, x_peer)
    c.start()
    c.wait()
    part = out.at[pl.ds(core * 16, 16)]
    c = copy(part, part, gc_send, gc_recv, core_peer)
    c.start()
    c.wait()


def sums(packed):
    dma = pltpu.SemaphoreType.DMA
    return pl.pallas_call(
        sums_kernel,
        out_shape=jax.ShapeDtypeStruct((LONS, SHARD, 128), BF16),
        in_specs=[vmem_spec()],
        out_specs=vmem_spec(),
        scratch_shapes=[
            pltpu.VMEM((16, SHARD, 128), BF16),
            pltpu.VMEM((8, SHARD, 128), BF16),
            pltpu.VMEM((Z - 1, SHARD, 128), BF16),
            pltpu.VMEM((LATS, WEIGHT_ROWS, 128), BF16),
            pltpu.VMEM((16, SHARD, 128), BF16),
            pltpu.VMEM((WEIGHT_ROWS, 128), BF16),
            dma, dma, dma, dma,
            dma((Z - 1,)), dma((Z - 1,)), dma((LATS - 1,)), dma((LATS - 1,)),
            dma((Z - 1,)), dma((Z - 1,)), dma((Z - 1,)), dma((Z - 1,)),
            dma, dma, dma, dma,
        ],
        compiler_params=params(collective_id=2, has_side_effects=True),
        name="sums",
    )(packed)


def unpack_kernel(src, bias_ref, qkv_ref, out_ref, gain_ref, flat, weight):
    for s in range(LONS):
        flat[s * BIAS_ROWS : (s + 1) * BIAS_ROWS, :] = src[s, :BIAS_ROWS, :].astype(F32)
    for s in range(16):
        weight[s * 48 : (s + 1) * 48, :128] = src[s, BIAS_ROWS:, :].astype(F32)
    for s in range(8):
        pair = src[16 + s, BIAS_ROWS:, :].astype(F32)
        weight[s * 48 : (s + 1) * 48, 128:] = pair[:, :64]
        weight[384 + s * 48 : 384 + (s + 1) * 48, 128:] = pair[:, 64:]
    gain = src[24, BIAS_ROWS : BIAS_ROWS + 16, :].astype(F32)
    gain_ref[:, :128] = gain[0:1, :]
    gain_ref[:, 128:] = gain[1:2, :64]
    qkv_ref[...] = jnp.transpose(weight[: 3 * WIDTH, :])
    out_ref[...] = weight[3 * WIDTH :, :]
    column = lax.broadcasted_iota(jnp.int32, (HALF, TOKENS), 1)
    for g in range(2):
        for w in range(2):
            rows = (TOKENS, HALF)[w]
            at = g * 1512 + w * 1008
            tail = flat[at + HEADS * rows : at + (HEADS + 1) * rows, :]
            for h in range(HEADS):
                main = flat[at + h * rows : at + (h + 1) * rows, :]
                value = jnp.concatenate([main, tail[:, 16 * h : 16 * h + 16]], axis=1)
                if w == 0:
                    bias_ref[g, w, h] = value
                else:
                    bias_ref[g, w, h, :HALF, :] = jnp.where(column < HALF, value, 0.0)
                    bias_ref[g, w, h, HALF:, :] = jnp.where(column < HALF, 0.0, value)


def unpack(src):
    return pl.pallas_call(
        unpack_kernel,
        out_shape=(
            jax.ShapeDtypeStruct((2, 2, HEADS, TOKENS, TOKENS), F32),
            jax.ShapeDtypeStruct((WIDTH, 3 * WIDTH), F32),
            jax.ShapeDtypeStruct((WIDTH, WIDTH), F32),
            jax.ShapeDtypeStruct((1, WIDTH), F32),
        ),
        in_specs=[vmem_spec()],
        out_specs=(vmem_spec(),) * 4,
        scratch_shapes=[pltpu.VMEM((BIAS_ALL, 128), F32), pltpu.VMEM((4 * WIDTH, WIDTH), F32)],
        compiler_params=params(),
        name="unpack",
    )(src)


def local(fields, out_grad, gain, qkv_weight, out_weight, window_bias):
    tables = window_bias.reshape(2, 2, HEADS, TOKENS, TOKENS)
    a, b = pack_in(fields, out_grad)
    a, b, c = halo(1, a, b)
    xw, gw = assemble(fields, out_grad, a, b, c)
    ig, packed = compute(xw, gw, gain, qkv_weight, out_weight, tables)
    tiles, e, d = pack_out(ig)
    e, d, f = halo(-1, e, d)
    input_grad = place(tiles, e, d, f)
    bias, qkv_grad, out_weight_grad, gain_grad = unpack(sums(packed))
    return (
        input_grad,
        qkv_grad,
        out_weight_grad,
        gain_grad.reshape(WIDTH),
        bias.reshape(2, 2, HEADS, TOKENS * TOKENS),
    )


def solution(mesh):
    in_specs = (
        P(None, "lat", "lon", None),
        P(None, "lat", "lon", None),
        P(),
        P(),
        P(),
        P("lat", None, None, None),
    )
    out_specs = (P(None, "lat", "lon", None), P(), P(), P(), P("lat", None, None, None))
    return jax.shard_map(local, mesh=mesh, in_specs=in_specs, out_specs=out_specs, check_vma=False)
```

```python
import jax
import jax.numpy as jnp
from jax import lax
from jax.experimental import pallas as pl
from jax.experimental.pallas import tpu as pltpu
from jax.sharding import PartitionSpec as P

F32 = jnp.float32
BF16 = jnp.bfloat16
MESH = pl.DeviceIdType.MESH

EPS = 1e-05
MASKED = -1e30
LOG2E = 1.4426950408889634

LEVELS = 4
ROWS = 24
COLS = 12
WIDTH = 192
HEADS = 6
HEAD = 32
TOKENS = 144
HALF = 72
LATS = 8
LONS = 32
Z = 8

CHUNK_ROWS = (32, 16, 32, 16, 48)
BIAS_CHUNKS = ((1, 0), (1, 1), (0, 0), (0, 1))
WEIGHTS = 4

VMEM_LIMIT = 56 * 1024 * 1024


def dot(a, b, contract=(1, 0)):
    return lax.dot_general(
        a, b, (((contract[0],), (contract[1],)), ((), ())), preferred_element_type=F32
    )


def remote(source, target, send, recv, there):
    return pltpu.make_async_remote_copy(
        src_ref=source, dst_ref=target, send_sem=send, recv_sem=recv, device_id=there, device_id_type=MESH
    )


def put_cells(own, tiles_of, win, g, k, lat):
    @pl.loop(0, LEVELS)
    def _(z):
        lev = (z + 1) % LEVELS
        w, zl = z // 2, z % 2
        for lp in range(12):
            row = 12 * g + lp - 6
            at = lp * 6
            if row >= ROWS:
                win[k, w, g, 0, zl, at : at + 6, :] = jnp.zeros((6, WIDTH), F32)
                win[k, w, g, 1, zl, at : at + 6, :] = jnp.zeros((6, WIDTH), F32)
                continue
            if row < 0:
                tile = tiles_of[lev, (row + 6) * 12 : (row + 6) * 12 + 12, k * WIDTH : (k + 1) * WIDTH].astype(F32)
                tile = jnp.where(lat == 0, 0.0, tile)
            else:
                tile = own[lev, row].astype(F32)
            win[k, w, g, 0, zl, at : at + 6, :] = tile[3:9]
            win[k, w, g, 1, zl, at : at + 3, :] = tile[9:12]


def put_east(east, corner, win, g, k, lat):
    @pl.loop(0, LEVELS)
    def _(z):
        lev = (z + 1) % LEVELS
        w, zl = z // 2, z % 2
        lanes = slice(k * WIDTH, (k + 1) * WIDTH)
        for lp in range(12):
            row = 12 * g + lp - 6
            if row >= ROWS:
                continue
            if row < 0:
                cells = corner[lev, (row + 6) * 3 : (row + 6) * 3 + 3, lanes]
                cells = jnp.where(lat == 0, 0.0, cells)
            else:
                at = ((row - 18) % ROWS) * 3
                cells = east[lev, at : at + 3, lanes]
            win[k, w, g, 1, zl, lp * 6 + 3 : lp * 6 + 6, :] = cells


def window(win, w, g, n, gain, qkv_ref, qkv_t_ref, out_ref, masked, bias_acc, weight_acc, gain_acc):
    scale = HEAD ** (-0.5)
    x = win[0, w, g, n].reshape(TOKENS, WIDTH)
    centred = x - jnp.mean(x, axis=-1, keepdims=True)
    inv_std = lax.rsqrt(jnp.mean(centred * centred, axis=-1, keepdims=True) + EPS)
    standard = centred * inv_std
    normed = (standard * gain).astype(BF16)
    upstream32 = win[1, w, g, n].reshape(TOKENS, WIDTH)
    upstream = upstream32.astype(BF16)
    projected = dot(normed, qkv_ref[...]).astype(BF16)
    queries_t = dot(qkv_t_ref[:WIDTH, :], normed, (1, 1)).astype(BF16)
    attended_grad = dot(upstream, out_ref[...], (1, 1)).astype(BF16)
    attended_grad_t = dot(out_ref[...], upstream, (1, 1)).astype(BF16)
    lane = lax.broadcasted_iota(jnp.int32, (TOKENS, WIDTH), 1)
    own = [(lane // HEAD) == h for h in range(HEADS)]
    zero = jnp.zeros((), BF16)
    queries_all = jnp.concatenate([jnp.where(own[h], projected[:, :WIDTH], zero) for h in range(HEADS)], axis=0)
    upper_all = jnp.concatenate([jnp.where(own[h], attended_grad, zero) for h in range(HEADS)], axis=0)
    keys = projected[:, WIDTH : 2 * WIDTH]
    values = projected[:, 2 * WIDTH :]
    scores_all = dot(queries_all, keys, (1, 1))
    grads_all = dot(upper_all, values, (1, 1))
    keys_parts, values_parts, lows, scores_lows = [], [], [], []
    for h in range(HEADS):
        at = slice(h * TOKENS, (h + 1) * TOKENS)
        rows = slice(h * HEAD, (h + 1) * HEAD)
        scores = scores_all[at] * (scale * LOG2E) + masked[h]
        exps = jnp.exp2(scores - jnp.max(scores, axis=-1, keepdims=True))
        attention = exps * (1.0 / jnp.sum(exps, axis=-1, keepdims=True))
        low = attention.astype(BF16)
        attention_grad = grads_all[at]
        delta = jnp.sum(attention * attention_grad, axis=-1, keepdims=True)
        scores_grad = attention * (attention_grad - delta)
        bias_acc[h] += scores_grad
        scores_low = scores_grad.astype(BF16)
        lows.append(low)
        scores_lows.append(scores_low)
        values_parts.append(dot(attended_grad_t[rows], low).astype(BF16))
        keys_parts.append((dot(queries_t[rows], scores_low) * scale).astype(BF16))
    attended_all = dot(jnp.concatenate(lows, axis=0), values)
    queries_grad_all = dot(jnp.concatenate(scores_lows, axis=0), keys)
    attended_sum = jnp.zeros((TOKENS, WIDTH), F32)
    queries_sum = jnp.zeros((TOKENS, WIDTH), F32)
    for h in range(HEADS):
        at = slice(h * TOKENS, (h + 1) * TOKENS)
        attended_sum = jnp.where(own[h], attended_all[at], attended_sum)
        queries_sum = jnp.where(own[h], queries_grad_all[at], queries_sum)
    attended_t = jnp.transpose(attended_sum).astype(BF16)
    queries_grad_t = (jnp.transpose(queries_sum) * scale).astype(BF16)
    projected_grad_t = jnp.concatenate([queries_grad_t] + keys_parts + values_parts, axis=0)
    weight_acc[3 * WIDTH :, :] += dot(attended_t, upstream)
    weight_acc[: 3 * WIDTH, :] += dot(projected_grad_t, normed)
    shifted_t = dot(qkv_ref[...], projected_grad_t)
    grad = jnp.transpose(shifted_t).astype(BF16).astype(F32)
    product = grad * standard
    gain_acc[...] += jnp.sum(product, axis=0, keepdims=True)
    scaled = grad * gain
    ig = upstream32 + inv_std * (
        scaled
        - jnp.mean(scaled, axis=-1, keepdims=True)
        - standard * jnp.mean(product * gain, axis=-1, keepdims=True)
    )
    win[0, w, g, n] = ig.reshape(2, HALF, WIDTH)


def mask_bias(masked, bias_ref, w, g, lat):
    q = lax.broadcasted_iota(jnp.int32, (TOKENS, 1), 0)
    k = lax.broadcasted_iota(jnp.int32, (1, TOKENS), 1)
    half = ((q >= HALF) != (k >= HALF)) & (w == 1)
    q_low = ((q // 6) % 12) < 6
    k_low = ((k // 6) % 12) < 6
    top = (q_low | k_low) & (g == 0) & (lat == 0)
    bottom = jnp.logical_not(q_low & k_low) & (g == 2)
    blocked = half | top | bottom
    table = jnp.minimum(g, 1)
    for h in range(HEADS):
        masked[h] = jnp.where(blocked, MASKED, bias_ref[table, w, h] * LOG2E)


def fold(w, take, flat, src):
    rows = (TOKENS, HALF)[w]
    tails = []
    for h in range(HEADS):
        value = take(h)
        flat[h * rows : (h + 1) * rows, :] = value[:, :128]
        tails.append(value[:, 128:])
    tails.append(jnp.zeros((rows, 32), F32))
    flat[HEADS * rows : 7 * rows, :] = jnp.concatenate(tails, axis=1)
    flat[7 * rows : 7 * rows + (16, 8)[w], :] = jnp.zeros(((16, 8)[w], 128), F32)
    each = (32, 16)[w]
    src[...] = flat[: LONS * each, :].astype(BF16).reshape(LONS, each, 128)


def fold_weights(weight_acc, gain_acc, src):
    for s in range(16):
        src[s] = weight_acc[s * 48 : (s + 1) * 48, :128].astype(BF16)
    for s in range(8):
        pair = jnp.concatenate(
            [weight_acc[s * 48 : (s + 1) * 48, 128:], weight_acc[384 + s * 48 : 384 + (s + 1) * 48, 128:]], axis=1
        )
        src[16 + s] = pair.astype(BF16)
    total = gain_acc[...]
    left = jnp.broadcast_to(total[:, :128], (48, 128))
    right = jnp.concatenate([total[:, 128:], jnp.zeros((1, 64), F32)], axis=1)
    right = jnp.broadcast_to(right, (48, 128))
    row = lax.broadcasted_iota(jnp.int32, (48, 128), 0)
    src[24] = jnp.where(row == 0, left, jnp.where(row == 1, right, 0.0)).astype(BF16)
    src[25:] = jnp.zeros((LONS - 25, 48, 128), BF16)


def unfold(w, out, flat, bias_out):
    rows, each = (TOKENS, HALF)[w], (32, 16)[w]
    flat[: LONS * each, :] = out[...].reshape(LONS * each, 128).astype(F32)
    tail = flat[HEADS * rows : 7 * rows, :]
    column = lax.broadcasted_iota(jnp.int32, (HALF, TOKENS), 1)
    for h in range(HEADS):
        value = jnp.concatenate([flat[h * rows : (h + 1) * rows, :], tail[:, 16 * h : 16 * h + 16]], axis=1)
        if w == 0:
            bias_out[h] = value
        else:
            bias_out[h, :HALF, :] = jnp.where(column < HALF, value, 0.0)
            bias_out[h, HALF:, :] = jnp.where(column < HALF, 0.0, value)


def unfold_weights(out, weight, qkv_ref, out_ref, gain_ref):
    for s in range(16):
        weight[s * 48 : (s + 1) * 48, :128] = out[s].astype(F32)
    for s in range(8):
        pair = out[16 + s].astype(F32)
        weight[s * 48 : (s + 1) * 48, 128:] = pair[:, :64]
        weight[384 + s * 48 : 384 + (s + 1) * 48, 128:] = pair[:, 64:]
    gain = out[24, 0:16, :].astype(F32)
    gain_ref[:, :128] = gain[0:1, :]
    gain_ref[:, 128:] = gain[1:2, :64]
    qkv_ref[...] = jnp.transpose(weight[: 3 * WIDTH, :])
    out_ref[...] = weight[3 * WIDTH :, :]


def kernel(
    fields_hbm, grad_hbm, gain_ref, qkv_ref, qkv_t_ref, out_w_ref, bias_hbm,
    input_grad_hbm, qkv_grad_ref, out_grad_ref, gain_grad_ref, bias_grad_hbm,
    fields, grads, bias, bias_out, cells_out,
    a_send, b_send, a_recv, b_recv, c_recv, pack32, east32, corner32,
    win, masked, bias_acc, weight_acc, gain_acc, flat,
    tiles, e_send, d_send, e_recv, d_recv, f_recv,
    src0, src1, src2, src3, src4, core0, core1, core2, core3, core4,
    xb0, xb1, xb2, xb3, xb4, zb0, zb1, zb2, zb3, zb4, out0, out1, out2, out3, out4,
    lat_send_buf, lat_buf,
    local_sem, halo_send, halo_recv, pair_send, pair_recv, z_send, z_recv, gz_send, gz_recv, lat_send, lat_recv,
):
    lat = lax.axis_index("lat")
    lon = lax.axis_index("lon")
    last = lat == LATS - 1
    z, x, core = lon // 4, (lon // 2) % 2, lon % 2
    up, down = (lat + LATS - 1) % LATS, (lat + 1) % LATS
    west, east = (lon + LONS - 1) % LONS, (lon + 1) % LONS

    def at_lon(zz, xx, cc):
        return (lat, zz * 4 + xx * 2 + cc)

    core_peer = at_lon(z, x, 1 - core)
    x_peer = at_lon(z, 1 - x, core)
    z_peers = [at_lon((z + d) % Z, x, core) for d in range(1, Z)]
    lat_peers = [((lat + d) % LATS, lon) for d in range(1, LATS)]

    loads = [
        pltpu.make_async_copy(fields_hbm, fields, local_sem.at[0]),
        pltpu.make_async_copy(grad_hbm, grads, local_sem.at[1]),
        pltpu.make_async_copy(bias_hbm, bias, local_sem.at[2]),
    ]
    for c in loads:
        c.start()
    barrier = pltpu.get_barrier_semaphore()
    greeted = [core_peer, x_peer, (lat, west), (lat, east), (down, west), (up, east)] + z_peers + lat_peers
    for there in greeted:
        pl.semaphore_signal(barrier, inc=1, device_id=there, device_id_type=MESH)

    loads[0].wait()
    loads[1].wait()

    @pl.loop(0, LEVELS)
    def _(lev):
        for k, own in enumerate((fields, grads)):
            for r in range(ROWS):
                at = ((r - 18) % ROWS) * 3
                pack32[lev, at : at + 3, k * WIDTH : (k + 1) * WIDTH] = own[lev, r].astype(F32)[0:3]
        b_send[lev] = pack32[lev, 0:80].astype(BF16)
        for k, own in enumerate((fields, grads)):
            for r in range(6):
                pack32[lev, r * 12 : r * 12 + 12, k * WIDTH : (k + 1) * WIDTH] = own[lev, 18 + r].astype(F32)
        a_send[lev] = pack32[lev, 0:80].astype(BF16)

    pl.semaphore_wait(barrier, len(greeted))
    b_copy = remote(b_send, b_recv, halo_send.at[0], halo_recv.at[0], (lat, west))
    a_copy = remote(a_send, a_recv, halo_send.at[1], halo_recv.at[1], (down, lon))
    c_copy = remote(b_send.at[:, 0:32], c_recv, halo_send.at[2], halo_recv.at[2], (down, west))
    b_copy.start()

    @pl.when(lat < LATS - 1)
    def _():
        a_copy.start()
        c_copy.start()

    weight_acc[...] = jnp.zeros_like(weight_acc)
    gain_acc[...] = jnp.zeros_like(gain_acc)
    for k, own in enumerate((fields, grads)):
        for g in (1, 2):
            put_cells(own, a_recv, win, g, k, lat)
    loads[2].wait()
    b_copy.wait()
    east32[...] = b_recv[...].astype(F32)
    for k in range(2):
        for g in (1, 2):
            put_east(east32, corner32, win, g, k, lat)

    srcs = (src0, src1, src2, src3, src4)
    core_bufs = (core0, core1, core2, core3, core4)
    x_bufs = (xb0, xb1, xb2, xb3, xb4)
    z_bufs = (zb0, zb1, zb2, zb3, zb4)
    outs = (out0, out1, out2, out3, out4)
    mine = core * 16 + x * 8 + z

    def core_copy(c):
        return remote(
            srcs[c].at[pl.ds((1 - core) * 16, 16)], core_bufs[c], pair_send.at[c, 0], pair_recv.at[c, 0], core_peer
        )

    def x_copy(c):
        return remote(
            srcs[c].at[pl.ds(core * 16 + (1 - x) * 8, 8)], x_bufs[c], pair_send.at[c, 1], pair_recv.at[c, 1], x_peer
        )

    def z_copies(c):
        return [
            remote(
                srcs[c].at[core * 16 + x * 8 + (z + d) % Z], z_bufs[c].at[d - 1],
                z_send.at[c, d - 1], z_recv.at[c, d - 1], z_peers[d - 1],
            )
            for d in range(1, Z)
        ]

    def gz_copies(c):
        part = outs[c].at[mine]
        return [remote(part, part, gz_send.at[c, d - 1], gz_recv.at[c, d - 1], z_peers[d - 1]) for d in range(1, Z)]

    def gx_copy(c):
        part = outs[c].at[pl.ds(core * 16 + x * 8, 8)]
        return remote(part, part, pair_send.at[c, 2], pair_recv.at[c, 2], x_peer)

    def gc_copy(c):
        part = outs[c].at[pl.ds(core * 16, 16)]
        return remote(part, part, pair_send.at[c, 3], pair_recv.at[c, 3], core_peer)

    lat_copies = [
        remote(lat_send_buf, lat_buf.at[lat], lat_send.at[d - 1], lat_recv.at[d - 1], lat_peers[d - 1])
        for d in range(1, LATS)
    ]

    def start(copies):
        for c in copies:
            c.start()

    def wait(copies):
        for c in copies:
            c.wait()

    def add_core(c):
        core_copy(c).wait()
        half = pl.ds(core * 16, 16)
        srcs[c][half] = (srcs[c][half].astype(F32) + core_bufs[c][...].astype(F32)).astype(BF16)
        x_copy(c).start()

    def add_x(c):
        x_copy(c).wait()
        part = pl.ds(core * 16 + x * 8, 8)
        srcs[c][part] = (srcs[c][part].astype(F32) + x_bufs[c][...].astype(F32)).astype(BF16)
        start(z_copies(c))

    def add_z(c):
        wait(z_copies(c))
        total = srcs[c][mine].astype(F32)
        for d in range(Z - 1):
            total = total + z_bufs[c][d].astype(F32)
        return total.astype(BF16)

    def gather_z(c):
        outs[c][mine] = add_z(c)
        start(gz_copies(c))

    def gather_x(c):
        wait(gz_copies(c))
        gx_copy(c).start()

    def gather_core(c):
        gx_copy(c).wait()
        gc_copy(c).start()

    def bias_store(c):
        g, w = BIAS_CHUNKS[c]
        return pltpu.make_async_copy(bias_out.at[g, w], bias_grad_hbm.at[g, w], local_sem.at[3 + c])

    def finish(c):
        gc_copy(c).wait()
        g, w = BIAS_CHUNKS[c]
        unfold(w, outs[c], flat, bias_out.at[g, w])
        bias_store(c).start()

    @pl.loop(0, 6)
    def _(t):
        early = jnp.where(t < 4, 1, 0)
        g = early * (2 - t % 2)
        w = early * (t // 2) + (1 - early) * (t - 4)

        @pl.when(t == 4)
        def _():
            @pl.when(lat < LATS - 1)
            def _():
                a_copy.wait_send()
                c_copy.wait_send()

            @pl.when(lat > 0)
            def _():
                a_copy.wait_recv()
                c_copy.wait_recv()

            corner32[...] = c_recv[...].astype(F32)
            for k, own in enumerate((fields, grads)):
                put_cells(own, a_recv, win, 0, k, lat)
                put_east(east32, corner32, win, 0, k, lat)

        @pl.when((t == 0) | (t == 2) | (t >= 4))
        def _():
            bias_acc[...] = jnp.zeros_like(bias_acc)

        @pl.when((g < 2) | last)
        def _():
            mask_bias(masked, bias, w, g, lat)
            gain = gain_ref[...]
            for n in range(2):
                window(win, w, g, n, gain, qkv_ref, qkv_t_ref, out_w_ref, masked, bias_acc, weight_acc, gain_acc)

        @pl.when(t == 1)
        def _():
            fold(0, lambda h: bias_acc[h], flat, src0)
            core_copy(0).start()

        @pl.when(t == 3)
        def _():
            fold(1, lambda h: bias_acc[h, :HALF, :] + bias_acc[h, HALF:, :], flat, src1)
            core_copy(1).start()
            add_core(0)

        @pl.when(t == 4)
        def _():
            fold(0, lambda h: bias_acc[h], flat, src2)
            core_copy(2).start()
            add_core(1)
            add_x(0)

        @pl.when(t == 5)
        def _():
            fold_weights(weight_acc, gain_acc, src4)
            core_copy(4).start()
            fold(1, lambda h: bias_acc[h, :HALF, :] + bias_acc[h, HALF:, :], flat, src3)
            core_copy(3).start()
            add_core(2)
            add_x(1)
            gather_z(0)


    add_core(4)
    add_core(3)

    @pl.loop(0, LEVELS)
    def _(zz):
        lev = (zz + 1) % LEVELS
        w, zl = zz // 2, zz % 2
        for g in range(3):
            for lp in range(12 if g < 2 else 6):
                at, r = lp * 6, 12 * g + lp
                tiles[lev, r, 3:9, :] = win[0, w, g, 0, zl, at : at + 6, :]
                tiles[lev, r, 9:12, :] = win[0, w, g, 1, zl, at : at + 3, :]
                pack32[lev, r * 3 : r * 3 + 3, 0:WIDTH] = win[0, w, g, 1, zl, at + 3 : at + 6, :]
        d_send[lev] = pack32[lev, :, 0:WIDTH].astype(BF16)
        for r in range(6):
            pack32[lev, r * 12 : r * 12 + 12, 0:WIDTH] = tiles[lev, r]
        e_send[lev] = pack32[lev, 0:80, 0:WIDTH].astype(BF16)

    d_copy = remote(d_send, d_recv, halo_send.at[3], halo_recv.at[3], (lat, east))
    e_copy = remote(e_send, e_recv, halo_send.at[4], halo_recv.at[4], (up, lon))
    f_copy = remote(d_send.at[:, 0:32], f_recv, halo_send.at[5], halo_recv.at[5], (up, east))
    d_copy.start()

    @pl.when(lat > 0)
    def _():
        e_copy.start()
        f_copy.start()

    add_x(2)
    gather_z(1)
    gather_x(0)
    add_x(4)
    add_x(3)
    gather_z(2)
    gather_x(1)
    gather_core(0)
    lat_send_buf[...] = add_z(4)
    lat_buf[lat] = lat_send_buf[...]
    start(lat_copies)
    gather_z(3)
    gather_x(2)
    gather_core(1)
    wait(lat_copies)
    total = lat_buf[0].astype(F32)
    for i in range(1, LATS):
        total = total + lat_buf[i].astype(F32)
    outs[4][mine] = total.astype(BF16)
    start(gz_copies(4))
    gather_x(3)
    gather_core(2)
    finish(0)

    d_copy.wait()

    @pl.when(lat > 0)
    def _():
        e_copy.wait_send()
        f_copy.wait_send()

    @pl.when(lat < LATS - 1)
    def _():
        e_copy.wait_recv()
        f_copy.wait_recv()

    column = lax.broadcasted_iota(jnp.int32, (COLS, WIDTH), 0)

    @pl.loop(0, LEVELS)
    def _(lev):
        pack32[lev, :, 0:WIDTH] = d_recv[lev].astype(F32)
        corner32[lev, :, 0:WIDTH] = f_recv[lev].astype(F32)
        for row in range(ROWS):
            if row < 18:
                own = tiles[lev, row + 6]
                from_west = pack32[lev, (row + 6) * 3 : (row + 6) * 3 + 3, 0:WIDTH]
            else:
                r = row - 18
                own = jnp.where(last, tiles[lev, 24 + r], e_recv[lev, r * 12 : r * 12 + 12, :].astype(F32))
                from_west = jnp.where(
                    last,
                    pack32[lev, (24 + r) * 3 : (24 + r) * 3 + 3, 0:WIDTH],
                    corner32[lev, r * 3 : r * 3 + 3, 0:WIDTH],
                )
            from_west = jnp.concatenate([from_west, jnp.zeros((COLS - 3, WIDTH), F32)], axis=0)
            cells_out[lev, row] = jnp.where(column < 3, from_west, own).astype(BF16)

    cells_store = pltpu.make_async_copy(cells_out, input_grad_hbm, local_sem.at[7])
    cells_store.start()
    gather_x(4)
    gather_core(3)
    finish(1)
    gather_core(4)
    finish(2)
    finish(3)
    gc_copy(4).wait()
    unfold_weights(outs[4], weight_acc, qkv_grad_ref, out_grad_ref, gain_grad_ref)
    for c in range(4):
        bias_store(c).wait()
    cells_store.wait()


def block(fields, out_grad, gain, qkv, out_weight, bias):
    dma = pltpu.SemaphoreType.DMA
    vmem = pl.BlockSpec(memory_space=pltpu.VMEM)
    hbm = pl.BlockSpec(memory_space=pl.ANY)

    def per_chunk(count):
        return [pltpu.VMEM((count, rows, 128), BF16) for rows in CHUNK_ROWS]

    return pl.pallas_call(
        kernel,
        out_shape=(
            jax.ShapeDtypeStruct((LEVELS, ROWS, COLS, WIDTH), BF16),
            jax.ShapeDtypeStruct((WIDTH, 3 * WIDTH), F32),
            jax.ShapeDtypeStruct((WIDTH, WIDTH), F32),
            jax.ShapeDtypeStruct((1, WIDTH), F32),
            jax.ShapeDtypeStruct((2, 2, HEADS, TOKENS, TOKENS), F32),
        ),
        in_specs=[hbm, hbm, vmem, vmem, vmem, vmem, hbm],
        out_specs=(hbm, vmem, vmem, vmem, hbm),
        scratch_shapes=[
            pltpu.VMEM((LEVELS, ROWS, COLS, WIDTH), BF16),
            pltpu.VMEM((LEVELS, ROWS, COLS, WIDTH), BF16),
            pltpu.VMEM((2, 2, HEADS, TOKENS, TOKENS), F32),
            pltpu.VMEM((2, 2, HEADS, TOKENS, TOKENS), F32),
            pltpu.VMEM((LEVELS, ROWS, COLS, WIDTH), BF16),
            pltpu.VMEM((LEVELS, 80, 2 * WIDTH), BF16),
            pltpu.VMEM((LEVELS, 80, 2 * WIDTH), BF16),
            pltpu.VMEM((LEVELS, 80, 2 * WIDTH), BF16),
            pltpu.VMEM((LEVELS, 80, 2 * WIDTH), BF16),
            pltpu.VMEM((LEVELS, 32, 2 * WIDTH), BF16),
            pltpu.VMEM((LEVELS, 96, 2 * WIDTH), F32),
            pltpu.VMEM((LEVELS, 80, 2 * WIDTH), F32),
            pltpu.VMEM((LEVELS, 32, 2 * WIDTH), F32),
            pltpu.VMEM((2, 2, 3, 2, 2, HALF, WIDTH), F32),
            pltpu.VMEM((HEADS, TOKENS, TOKENS), F32),
            pltpu.VMEM((HEADS, TOKENS, TOKENS), F32),
            pltpu.VMEM((4 * WIDTH, WIDTH), F32),
            pltpu.VMEM((1, WIDTH), F32),
            pltpu.VMEM((1024, 128), F32),
            pltpu.VMEM((LEVELS, 30, COLS, WIDTH), F32),
            pltpu.VMEM((LEVELS, 80, WIDTH), BF16),
            pltpu.VMEM((LEVELS, 96, WIDTH), BF16),
            pltpu.VMEM((LEVELS, 80, WIDTH), BF16),
            pltpu.VMEM((LEVELS, 96, WIDTH), BF16),
            pltpu.VMEM((LEVELS, 32, WIDTH), BF16),
            *per_chunk(LONS),
            *per_chunk(16),
            *per_chunk(8),
            *per_chunk(Z - 1),
            *per_chunk(LONS),
            pltpu.VMEM((48, 128), BF16),
            pltpu.VMEM((LATS, 48, 128), BF16),
            dma((8,)), dma((6,)), dma((6,)), dma((5, 4)), dma((5, 4)),
            dma((5, Z - 1)), dma((5, Z - 1)), dma((5, Z - 1)), dma((5, Z - 1)),
            dma((LATS - 1,)), dma((LATS - 1,)),
        ],
        compiler_params=pltpu.CompilerParams(
            vmem_limit_bytes=VMEM_LIMIT, collective_id=0, has_side_effects=True
        ),
        name="block",
    )(fields, out_grad, gain.reshape(1, WIDTH), qkv, qkv.T, out_weight, bias)


def local(fields, out_grad, gain, qkv_weight, out_weight, window_bias):
    tables = window_bias.reshape(2, 2, HEADS, TOKENS, TOKENS)
    input_grad, qkv_grad, out_weight_grad, gain_grad, bias = block(
        fields, out_grad, gain, qkv_weight, out_weight, tables
    )
    return (
        input_grad,
        qkv_grad,
        out_weight_grad,
        gain_grad.reshape(WIDTH),
        bias.reshape(2, 2, HEADS, TOKENS * TOKENS),
    )


def solution(mesh):
    in_specs = (
        P(None, "lat", "lon", None),
        P(None, "lat", "lon", None),
        P(),
        P(),
        P(),
        P("lat", None, None, None),
    )
    out_specs = (P(None, "lat", "lon", None), P(), P(), P(), P("lat", None, None, None))
    return jax.shard_map(local, mesh=mesh, in_specs=in_specs, out_specs=out_specs, check_vma=False)
```

```python
import jax
import jax.numpy as jnp
from jax import lax
from jax.experimental import pallas as pl
from jax.experimental.layout import Layout, with_layout_constraint
from jax.experimental.pallas import tpu as pltpu
from jax.sharding import PartitionSpec as P

F32 = jnp.float32
BF16 = jnp.bfloat16
MESH = pl.DeviceIdType.MESH

EPS = 1e-05
MASKED = -1e30
LOG2E = 1.4426950408889634

LEVELS = 4
ROWS = 24
COLS = 12
WIDTH = 192
HEADS = 6
HEAD = 32
TOKENS = 144
HALF = 72
FLAT = 162
LATS = 8
LONS = 32
Z = 8

CHUNK_ROWS = (32, 16, 32, 16, 48)
BIAS_CHUNKS = ((1, 0), (1, 1), (0, 0), (0, 1))
WEIGHTS = 4

VMEM_LIMIT = 56 * 1024 * 1024


def dot(a, b, contract=(1, 0)):
    return lax.dot_general(
        a, b, (((contract[0],), (contract[1],)), ((), ())), preferred_element_type=F32
    )


def remote(source, target, send, recv, there):
    return pltpu.make_async_remote_copy(
        src_ref=source, dst_ref=target, send_sem=send, recv_sem=recv, device_id=there, device_id_type=MESH
    )


def place_of(c):
    return c // 6, c % 6


def put_rows(win, at, start, rows):
    k, w, g, n, zl = at
    count = rows.shape[0]
    where_to = pl.ds(start, count, stride=6)
    win[k, w, g, n, 0, zl, where_to, :] = rows[:, :128]
    win[k, w, g, n, 1, zl, where_to, :] = jnp.concatenate([rows[:, 128:], jnp.zeros((count, 64), F32)], axis=1)


def take_rows(win, at, start, count):
    k, w, g, n, zl = at
    where_from = pl.ds(start, count, stride=6)
    return jnp.concatenate(
        [win[k, w, g, n, 0, zl, where_from, :], win[k, w, g, n, 1, zl, where_from, :][:, :64]], axis=1
    )


def take_window(win, at):
    return jnp.concatenate(
        [win[(*at, 0)].reshape(TOKENS, 128), win[(*at, 1)].reshape(TOKENS, 128)[:, :64]], axis=1
    )


def put_cells(own, win, k):
    @pl.loop(0, LEVELS)
    def _(z):
        lev, w, zl = (z + 1) % LEVELS, z // 2, z % 2
        for c in range(9):
            n, lo = place_of(c)
            tile = own[lev, c + 3].astype(F32)
            put_rows(win, (k, w, 0, n, zl), 36 + lo, tile[0:6])
            put_rows(win, (k, w, 1, n, zl), lo, tile[6:18])
            put_rows(win, (k, w, 2, 0, zl), 36 * n + lo, tile[18:24])


def put_east(east, win, k):
    @pl.loop(0, LEVELS)
    def _(z):
        lev, w, zl = (z + 1) % LEVELS, z // 2, z % 2
        for j in range(3):
            n, lo = place_of(9 + j)
            tile = east[k, lev, j].astype(F32)
            put_rows(win, (k, w, 0, n, zl), 36 + lo, tile[0:6])
            put_rows(win, (k, w, 1, n, zl), lo, tile[6:18])
            put_rows(win, (k, w, 2, 0, zl), 36 * n + lo, tile[18:24])


def put_above(above, corner, above32, corner32, win, lat):
    @pl.loop(0, LEVELS)
    def _(z):
        lev, w, zl = (z + 1) % LEVELS, z // 2, z % 2
        above32[lev, 0:64] = jnp.where(lat == 0, 0.0, above[lev].astype(F32))
        corner32[lev] = jnp.where(lat == 0, 0.0, corner[lev].astype(F32))
        for k in range(2):
            lanes = slice(k * WIDTH, (k + 1) * WIDTH)
            for c in range(12):
                n, lo = place_of(c)
                if c < 9:
                    cells = above32[lev, c * 6 : c * 6 + 6, lanes]
                else:
                    cells = corner32[lev, (c - 9) * 6 : (c - 9) * 6 + 6, lanes]
                put_rows(win, (k, w, 0, n, zl), lo, cells)


def window(win, w, g, n, gain, qkv_ref, query_t_ref, out_ref, masked, bias_acc, weight_acc, gain_acc):
    masked_lo, masked_hi = masked
    acc_lo, acc_hi = bias_acc
    scale = HEAD ** (-0.5)
    x = take_window(win, (0, w, g, n))
    centred = x - jnp.mean(x, axis=-1, keepdims=True)
    inv_std = lax.rsqrt(jnp.mean(centred * centred, axis=-1, keepdims=True) + EPS)
    standard = centred * inv_std
    normed = (standard * gain).astype(BF16)
    upstream32 = take_window(win, (1, w, g, n))
    upstream = upstream32.astype(BF16)
    projected = dot(normed, qkv_ref[...]).astype(BF16)
    queries_t = dot(query_t_ref[...], normed, (1, 1)).astype(BF16)
    attended_grad = dot(upstream, out_ref[...], (1, 1)).astype(BF16)
    attended_grad_t = dot(out_ref[...], upstream, (1, 1)).astype(BF16)
    lane = lax.broadcasted_iota(jnp.int32, (TOKENS, WIDTH), 1)
    own = [(lane // HEAD) == h for h in range(HEADS)]
    zero = jnp.zeros((), BF16)
    queries_all = jnp.concatenate([jnp.where(own[h], projected[:, :WIDTH], zero) for h in range(HEADS)], axis=0)
    upper_all = jnp.concatenate([jnp.where(own[h], attended_grad, zero) for h in range(HEADS)], axis=0)
    keys = projected[:, WIDTH : 2 * WIDTH]
    values = projected[:, 2 * WIDTH :]
    scores_all = dot(queries_all, keys, (1, 1))
    grads_all = dot(upper_all, values, (1, 1))
    keys_parts, values_parts, lows, scores_lows = [], [], [], []
    for h in range(HEADS):
        at = slice(h * TOKENS, (h + 1) * TOKENS)
        rows = slice(h * HEAD, (h + 1) * HEAD)
        table = jnp.concatenate([masked_lo[h], masked_hi[h, :, :16]], axis=1)
        scores = scores_all[at] * (scale * LOG2E) + table
        exps = jnp.exp2(scores - jnp.max(scores, axis=-1, keepdims=True))
        attention = exps * (1.0 / jnp.sum(exps, axis=-1, keepdims=True))
        low = attention.astype(BF16)
        attention_grad = grads_all[at]
        delta = jnp.sum(attention * attention_grad, axis=-1, keepdims=True)
        scores_grad = attention * (attention_grad - delta)
        acc_lo[h] += scores_grad[:, :128]
        acc_hi[h, :, :16] += scores_grad[:, 128:]
        scores_low = scores_grad.astype(BF16)
        lows.append(low)
        scores_lows.append(scores_low)
        values_parts.append(dot(attended_grad_t[rows], low).astype(BF16))
        keys_parts.append((dot(queries_t[rows], scores_low) * scale).astype(BF16))
    attended_all = dot(jnp.concatenate(lows, axis=0), values)
    queries_grad_all = dot(jnp.concatenate(scores_lows, axis=0), keys)
    attended_sum = jnp.zeros((TOKENS, WIDTH), F32)
    queries_sum = jnp.zeros((TOKENS, WIDTH), F32)
    for h in range(HEADS):
        at = slice(h * TOKENS, (h + 1) * TOKENS)
        attended_sum = jnp.where(own[h], attended_all[at], attended_sum)
        queries_sum = jnp.where(own[h], queries_grad_all[at], queries_sum)
    attended_t = jnp.transpose(attended_sum).astype(BF16)
    queries_grad_t = (jnp.transpose(queries_sum) * scale).astype(BF16)
    projected_grad_t = jnp.concatenate([queries_grad_t] + keys_parts + values_parts, axis=0)
    weight_acc[3 * WIDTH :, :] += dot(attended_t, upstream)
    weight_acc[: 3 * WIDTH, :] += dot(projected_grad_t, normed)
    shifted_t = dot(qkv_ref[...], projected_grad_t)
    grad = jnp.transpose(shifted_t).astype(BF16).astype(F32)
    product = grad * standard
    gain_acc[...] += jnp.sum(product, axis=0, keepdims=True)
    scaled = grad * gain
    ig = upstream32 + inv_std * (
        scaled
        - jnp.mean(scaled, axis=-1, keepdims=True)
        - standard * jnp.mean(product * gain, axis=-1, keepdims=True)
    )
    win[0, w, g, n, 0] = ig[:, :128].reshape(2, HALF, 128)
    win[0, w, g, n, 1, :, :, 0:64] = ig[:, 128:].reshape(2, HALF, 64)


def mask_bias(masked, bias_ref, w, g, lat):
    masked_lo, masked_hi = masked
    table = jnp.minimum(g, 1)
    lane = lax.broadcasted_iota(jnp.int32, (18, 128), 1)

    def low(token):
        return (token // 6) % 12 < 6

    for i in range(8):
        q = 8 * lax.broadcasted_iota(jnp.int32, (18, 1), 0) + i

        def blocked(k):
            half = ((q >= HALF) != (k >= HALF)) & (w == 1)
            top = (low(q) | low(k)) & (g == 0) & (lat == 0)
            bottom = (low(q) != low(k)) & (g == 2)
            return half | top | bottom

        k = lax.broadcasted_iota(jnp.int32, (1, 128), 1)
        blocked_lo, blocked_hi = blocked(k), blocked(k + 128)
        for h in range(HEADS):
            at = (table * HEADS + h) * (2 * FLAT) + w + 2 * i
            first = bias_ref[pl.ds(at, 18, stride=18), :]
            second = bias_ref[pl.ds(at + 2, 18, stride=18), :]
            lo = jnp.where(lane >= 16 * i, first, second)
            hi = second
            if i:
                lo = pltpu.roll(lo, 128 - 16 * i, 1)
                hi = pltpu.roll(hi, 128 - 16 * i, 1)
            masked_lo[h, pl.ds(i, 18, stride=8), :] = jnp.where(blocked_lo, MASKED, lo * LOG2E)
            masked_hi[h, pl.ds(i, 18, stride=8), :] = jnp.where(blocked_hi, MASKED, hi * LOG2E)


def double_mask(masked):
    masked_lo, masked_hi = masked
    k = lax.broadcasted_iota(jnp.int32, (36, 128), 1)
    own = (k // 6) % 12 >= 6
    for h in range(HEADS):
        for at in (0, HALF):
            rows = pltpu.roll(masked_lo[h, at : at + 36, :], 36, 1)
            masked_lo[h, at + 36 : at + 72, :] = jnp.where(own, rows, MASKED)
            masked_hi[h, at + 36 : at + 72, :] = rows


def join_sums(bias_acc):
    acc_lo, acc_hi = bias_acc
    lane = lax.broadcasted_iota(jnp.int32, (36, 128), 1)
    for h in range(HEADS):
        for at in (0, HALF):
            second = slice(at + 36, at + 72)
            lo, hi = pltpu.roll(acc_lo[h, second, :], 92, 1), pltpu.roll(acc_hi[h, second, :], 92, 1)
            acc_lo[h, at : at + 36, :] += jnp.where(lane < 92, lo, hi)
            acc_lo[h, second, :] = jnp.zeros((36, 128), F32)
            acc_hi[h, second, :] = jnp.zeros((36, 128), F32)


def fold(w, bias_acc, flat, src):
    acc_lo, acc_hi = bias_acc
    groups = (18, 9)[w]
    lane = lax.broadcasted_iota(jnp.int32, (groups, 128), 1)

    def take(ref, h, i):
        value = ref[h, pl.ds(i, groups, stride=8), :]
        return value + ref[h, pl.ds(HALF + i, groups, stride=8), :] if w else value

    for h in range(HEADS):
        before_lo = before_hi = None
        for i in range(9):
            if i < 8:
                lo, hi = take(acc_lo, h, i), take(acc_hi, h, i)
                if i:
                    lo, hi = pltpu.roll(lo, 16 * i, 1), pltpu.roll(hi, 16 * i, 1)
            rows = lo
            if i:
                rows = jnp.where(lane >= 16 * (i - 1), before_hi, before_lo)
                if i < 8:
                    rows = jnp.where(lane >= 16 * i, lo, rows)
            flat[pl.ds(h * 9 * groups + i, groups, stride=9), :] = rows
            before_lo, before_hi = lo, hi
    each = (32, 16)[w]
    flat[HEADS * 9 * groups : LONS * each, :] = jnp.zeros((LONS * each - HEADS * 9 * groups, 128), F32)
    src[...] = flat[: LONS * each, :].astype(BF16).reshape(LONS, each, 128)


def fold_weights(weight_acc, gain_acc, src):
    for s in range(16):
        src[s] = weight_acc[s * 48 : (s + 1) * 48, :128].astype(BF16)
    for s in range(8):
        pair = jnp.concatenate(
            [weight_acc[s * 48 : (s + 1) * 48, 128:], weight_acc[384 + s * 48 : 384 + (s + 1) * 48, 128:]], axis=1
        )
        src[16 + s] = pair.astype(BF16)
    total = gain_acc[...]
    left = jnp.broadcast_to(total[:, :128], (48, 128))
    right = jnp.concatenate([total[:, 128:], jnp.zeros((1, 64), F32)], axis=1)
    right = jnp.broadcast_to(right, (48, 128))
    row = lax.broadcasted_iota(jnp.int32, (48, 128), 0)
    src[24] = jnp.where(row == 0, left, jnp.where(row == 1, right, 0.0)).astype(BF16)
    src[25:] = jnp.zeros((LONS - 25, 48, 128), BF16)


def unfold(g, w, out, flat, bias_out):
    each = (32, 16)[w]
    flat[: LONS * each, :] = out[...].reshape(LONS * each, 128).astype(F32)
    row = lax.broadcasted_iota(jnp.int32, (81, 128), 0)
    lane = lax.broadcasted_iota(jnp.int32, (81, 128), 1)
    left = (128 * row + lane) % TOKENS < HALF
    for h in range(HEADS):
        at = (g * HEADS + h) * (2 * FLAT) + w
        if w == 0:
            bias_out[pl.ds(at, FLAT, stride=2), :] = flat[h * FLAT : (h + 1) * FLAT, :]
        else:
            rows = flat[h * 81 : (h + 1) * 81, :]
            bias_out[pl.ds(at, 81, stride=2), :] = jnp.where(left, rows, 0.0)
            bias_out[pl.ds(at + FLAT, 81, stride=2), :] = jnp.where(left, 0.0, rows)


def unfold_weights(out, weight, qkv_ref, out_ref, gain_ref):
    for s in range(16):
        weight[s * 48 : (s + 1) * 48, :128] = out[s].astype(F32)
    for s in range(8):
        pair = out[16 + s].astype(F32)
        weight[s * 48 : (s + 1) * 48, 128:] = pair[:, :64]
        weight[384 + s * 48 : 384 + (s + 1) * 48, 128:] = pair[:, 64:]
    gain = out[24, 0:16, :].astype(F32)
    gain_ref[:, :128] = gain[0:1, :]
    gain_ref[:, 128:] = gain[1:2, :64]
    qkv_ref[...] = jnp.transpose(weight[: 3 * WIDTH, :])
    out_ref[...] = weight[3 * WIDTH :, :]


def kernel(
    fields_hbm, grad_hbm, gain_ref, qkv_ref, out_w_ref, bias_hbm,
    input_grad_hbm, qkv_grad_ref, out_grad_ref, gain_grad_ref, bias_grad_hbm,
    fields, grads, bias, bias_out, cells_out, query_t,
    a_send, a_recv, b_recv, c_recv, pack32, corner32,
    win, masked_lo, masked_hi, acc_lo, acc_hi, weight_acc, gain_acc, flat,
    tiles, d_send, e_send, d_recv, e_recv, f_recv,
    src0, src1, src2, src3, src4, core0, core1, core2, core3, core4,
    xb0, xb1, xb2, xb3, xb4, zb0, zb1, zb2, zb3, zb4, out0, out1, out2, out3, out4,
    lat_send_buf, lat_buf,
    local_sem, halo_send, halo_recv, pair_send, pair_recv, z_send, z_recv, gz_send, gz_recv, lat_send, lat_recv,
):
    masked, bias_acc = (masked_lo, masked_hi), (acc_lo, acc_hi)
    lat = lax.axis_index("lat")
    lon = lax.axis_index("lon")
    last = lat == LATS - 1
    z, x, core = lon // 4, (lon // 2) % 2, lon % 2
    up, down = (lat + LATS - 1) % LATS, (lat + 1) % LATS
    west, east = (lon + LONS - 1) % LONS, (lon + 1) % LONS

    def at_lon(zz, xx, cc):
        return (lat, zz * 4 + xx * 2 + cc)

    core_peer = at_lon(z, x, 1 - core)
    x_peer = at_lon(z, 1 - x, core)
    z_peers = [at_lon((z + d) % Z, x, core) for d in range(1, Z)]
    lat_peers = [((lat + d) % LATS, lon) for d in range(1, LATS)]

    loads = [
        pltpu.make_async_copy(fields_hbm, fields, local_sem.at[0]),
        pltpu.make_async_copy(grad_hbm, grads, local_sem.at[1]),
        pltpu.make_async_copy(bias_hbm, bias, local_sem.at[2]),
    ]
    for c in loads:
        c.start()
    barrier = pltpu.get_barrier_semaphore()
    greeted = [core_peer, x_peer, (lat, west), (lat, east), (down, west), (up, east)] + z_peers + lat_peers
    for there in greeted:
        pl.semaphore_signal(barrier, inc=1, device_id=there, device_id_type=MESH)

    loads[0].wait()
    loads[1].wait()

    @pl.loop(0, LEVELS)
    def _(lev):
        for k, own in enumerate((fields, grads)):
            for col in range(COLS):
                at = (col - 3) * 6 if col >= 3 else 64 + col * 6
                pack32[lev, at : at + 6, k * WIDTH : (k + 1) * WIDTH] = own[lev, col].astype(F32)[18:24]
        a_send[lev] = pack32[lev].astype(BF16)

    pl.semaphore_wait(barrier, len(greeted))
    b_copies = [
        remote(own.at[:, 0:3], b_recv.at[k], halo_send.at[k], halo_recv.at[k], (lat, west))
        for k, own in enumerate((fields, grads))
    ]
    a_copy = remote(a_send.at[:, 0:64], a_recv, halo_send.at[2], halo_recv.at[2], (down, lon))
    c_copy = remote(a_send.at[:, 64:96], c_recv, halo_send.at[3], halo_recv.at[3], (down, west))
    for c in b_copies:
        c.start()

    @pl.when(lat < LATS - 1)
    def _():
        a_copy.start()
        c_copy.start()

    weight_acc[...] = jnp.zeros_like(weight_acc)
    gain_acc[...] = jnp.zeros_like(gain_acc)
    query_t[...] = jnp.transpose(qkv_ref[:, :WIDTH].astype(F32)).astype(BF16)
    for k, own in enumerate((fields, grads)):
        put_cells(own, win, k)
    loads[2].wait()
    for c in b_copies:
        c.wait()
    for k in range(2):
        put_east(b_recv, win, k)

    srcs = (src0, src1, src2, src3, src4)
    core_bufs = (core0, core1, core2, core3, core4)
    x_bufs = (xb0, xb1, xb2, xb3, xb4)
    z_bufs = (zb0, zb1, zb2, zb3, zb4)
    outs = (out0, out1, out2, out3, out4)
    mine = core * 16 + x * 8 + z

    def core_copy(c):
        return remote(
            srcs[c].at[pl.ds((1 - core) * 16, 16)], core_bufs[c], pair_send.at[c, 0], pair_recv.at[c, 0], core_peer
        )

    def x_copy(c):
        return remote(
            srcs[c].at[pl.ds(core * 16 + (1 - x) * 8, 8)], x_bufs[c], pair_send.at[c, 1], pair_recv.at[c, 1], x_peer
        )

    def z_copies(c):
        return [
            remote(
                srcs[c].at[core * 16 + x * 8 + (z + d) % Z], z_bufs[c].at[d - 1],
                z_send.at[c, d - 1], z_recv.at[c, d - 1], z_peers[d - 1],
            )
            for d in range(1, Z)
        ]

    def gz_copies(c):
        part = outs[c].at[mine]
        return [remote(part, part, gz_send.at[c, d - 1], gz_recv.at[c, d - 1], z_peers[d - 1]) for d in range(1, Z)]

    def gx_copy(c):
        part = outs[c].at[pl.ds(core * 16 + x * 8, 8)]
        return remote(part, part, pair_send.at[c, 2], pair_recv.at[c, 2], x_peer)

    def gc_copy(c):
        part = outs[c].at[pl.ds(core * 16, 16)]
        return remote(part, part, pair_send.at[c, 3], pair_recv.at[c, 3], core_peer)

    lat_copies = [
        remote(lat_send_buf, lat_buf.at[lat], lat_send.at[d - 1], lat_recv.at[d - 1], lat_peers[d - 1])
        for d in range(1, LATS)
    ]

    def start(copies):
        for c in copies:
            c.start()

    def wait(copies):
        for c in copies:
            c.wait()

    def add_core(c):
        core_copy(c).wait()
        half = pl.ds(core * 16, 16)
        srcs[c][half] = (srcs[c][half].astype(F32) + core_bufs[c][...].astype(F32)).astype(BF16)
        x_copy(c).start()

    def add_x(c):
        x_copy(c).wait()
        part = pl.ds(core * 16 + x * 8, 8)
        srcs[c][part] = (srcs[c][part].astype(F32) + x_bufs[c][...].astype(F32)).astype(BF16)
        start(z_copies(c))

    def add_z(c):
        wait(z_copies(c))
        total = srcs[c][mine].astype(F32)
        for d in range(Z - 1):
            total = total + z_bufs[c][d].astype(F32)
        return total.astype(BF16)

    def gather_z(c):
        outs[c][mine] = add_z(c)
        start(gz_copies(c))

    def gather_x(c):
        wait(gz_copies(c))
        gx_copy(c).start()

    def gather_core(c):
        gx_copy(c).wait()
        gc_copy(c).start()

    def bias_store(g):
        part = pl.ds(g * 2 * HEADS * FLAT, 2 * HEADS * FLAT)
        return pltpu.make_async_copy(bias_out.at[part], bias_grad_hbm.at[part], local_sem.at[3 + g])

    def finish(c):
        gc_copy(c).wait()
        g, w = BIAS_CHUNKS[c]
        unfold(g, w, outs[c], flat, bias_out)
        if w:
            bias_store(g).start()

    @pl.loop(0, 6)
    def _(t):
        early = jnp.where(t < 4, 1, 0)
        g = early * (2 - t % 2)
        w = early * (t // 2) + (1 - early) * (t - 4)

        @pl.when(t == 4)
        def _():
            @pl.when(lat < LATS - 1)
            def _():
                a_copy.wait_send()
                c_copy.wait_send()

            @pl.when(lat > 0)
            def _():
                a_copy.wait_recv()
                c_copy.wait_recv()

            put_above(a_recv, c_recv, pack32, corner32, win, lat)

        @pl.when((t == 0) | (t == 2) | (t >= 4))
        def _():
            acc_lo[...] = jnp.zeros_like(acc_lo)
            acc_hi[...] = jnp.zeros_like(acc_hi)

        def run(n):
            window(
                win, w, g, n, gain_ref[...], qkv_ref, query_t, out_w_ref, masked, bias_acc, weight_acc, gain_acc
            )

        @pl.when((g == 2) & last)
        def _():
            mask_bias(masked, bias, w, g, lat)
            double_mask(masked)
            run(0)
            join_sums(bias_acc)

        @pl.when(g < 2)
        def _():
            mask_bias(masked, bias, w, g, lat)
            run(0)
            run(1)

        @pl.when(t == 1)
        def _():
            fold(0, bias_acc, flat, src0)
            core_copy(0).start()

        @pl.when(t == 3)
        def _():
            fold(1, bias_acc, flat, src1)
            core_copy(1).start()
            add_core(0)

        @pl.when(t == 4)
        def _():
            fold(0, bias_acc, flat, src2)
            core_copy(2).start()
            add_core(1)
            add_x(0)

        @pl.when(t == 5)
        def _():
            fold_weights(weight_acc, gain_acc, src4)
            core_copy(4).start()
            fold(1, bias_acc, flat, src3)
            core_copy(3).start()
            add_core(2)
            add_x(1)
            gather_z(0)


    add_core(4)
    add_core(3)

    @pl.loop(0, LEVELS)
    def _(zz):
        lev, w, zl = (zz + 1) % LEVELS, zz // 2, zz % 2
        for c in range(COLS):
            n, lo = place_of(c)
            col = (c + 3) % COLS
            tiles[lev, col, 0:6, :] = take_rows(win, (0, w, 0, n, zl), 36 + lo, 6)
            tiles[lev, col, 6:18, :] = take_rows(win, (0, w, 1, n, zl), lo, 12)
            tiles[lev, col, 18:24, :] = take_rows(win, (0, w, 2, 0, zl), 36 * n + lo, 6)
            if c >= 9:
                d_send[lev, col] = tiles[lev, col].astype(BF16)
            at = c * 6 if c < 9 else 64 + (c - 9) * 6
            pack32[lev, at : at + 6, 0:WIDTH] = take_rows(win, (0, w, 0, n, zl), lo, 6)
        e_send[lev] = pack32[lev, :, 0:WIDTH].astype(BF16)

    d_copy = remote(d_send, d_recv, halo_send.at[4], halo_recv.at[4], (lat, east))
    e_copy = remote(e_send.at[:, 0:64], e_recv, halo_send.at[5], halo_recv.at[5], (up, lon))
    f_copy = remote(e_send.at[:, 64:96], f_recv, halo_send.at[6], halo_recv.at[6], (up, east))
    d_copy.start()

    @pl.when(lat > 0)
    def _():
        e_copy.start()
        f_copy.start()

    add_x(4)
    add_x(3)
    add_x(2)
    gather_z(1)
    gather_x(0)
    lat_send_buf[...] = add_z(4)
    lat_buf[lat] = lat_send_buf[...]
    start(lat_copies)
    gather_z(3)
    gather_z(2)
    gather_x(1)
    gather_core(0)
    wait(lat_copies)
    total = lat_buf[0].astype(F32)
    for i in range(1, LATS):
        total = total + lat_buf[i].astype(F32)
    outs[4][mine] = total.astype(BF16)
    start(gz_copies(4))
    gather_x(3)
    gather_x(2)
    gather_core(1)
    finish(0)
    gather_x(4)
    finish(1)
    gather_core(3)
    gather_core(2)

    d_copy.wait()

    @pl.when(lat > 0)
    def _():
        e_copy.wait_send()
        f_copy.wait_send()

    @pl.when(lat < LATS - 1)
    def _():
        e_copy.wait_recv()
        f_copy.wait_recv()

    gather_core(4)

    @pl.loop(0, LEVELS)
    def _(lev):
        pack32[lev, 0:64, 0:WIDTH] = e_recv[lev].astype(F32)
        corner32[lev, :, 0:WIDTH] = f_recv[lev].astype(F32)
        for col in range(COLS):
            if col < 3:
                tiles[lev, col] = d_recv[lev, col].astype(F32)
                cells = corner32[lev, col * 6 : col * 6 + 6, 0:WIDTH]
            else:
                cells = pack32[lev, (col - 3) * 6 : (col - 3) * 6 + 6, 0:WIDTH]
            tiles[lev, col, 18:24, :] = jnp.where(last, tiles[lev, col, 18:24, :], cells)
            cells_out[lev, col] = tiles[lev, col].astype(BF16)

    cells_store = pltpu.make_async_copy(cells_out, input_grad_hbm, local_sem.at[7])
    cells_store.start()
    finish(2)
    finish(3)
    gc_copy(4).wait()
    unfold_weights(outs[4], weight_acc, qkv_grad_ref, out_grad_ref, gain_grad_ref)
    for g in range(2):
        bias_store(g).wait()
    cells_store.wait()


def block(fields, out_grad, gain, qkv, out_weight, bias):
    dma = pltpu.SemaphoreType.DMA
    vmem = pl.BlockSpec(memory_space=pltpu.VMEM)
    hbm = pl.BlockSpec(memory_space=pl.ANY)

    def per_chunk(count):
        return [pltpu.VMEM((count, rows, 128), BF16) for rows in CHUNK_ROWS]

    cells = (LEVELS, COLS, ROWS, WIDTH)
    tables = (2 * 2 * HEADS * FLAT, 128)
    return pl.pallas_call(
        kernel,
        out_shape=(
            jax.ShapeDtypeStruct(cells, BF16),
            jax.ShapeDtypeStruct((WIDTH, 3 * WIDTH), F32),
            jax.ShapeDtypeStruct((WIDTH, WIDTH), F32),
            jax.ShapeDtypeStruct((1, WIDTH), F32),
            jax.ShapeDtypeStruct(tables, F32),
        ),
        in_specs=[hbm, hbm, vmem, vmem, vmem, hbm],
        out_specs=(hbm, vmem, vmem, vmem, hbm),
        scratch_shapes=[
            pltpu.VMEM(cells, BF16),
            pltpu.VMEM(cells, BF16),
            pltpu.VMEM(tables, F32),
            pltpu.VMEM(tables, F32),
            pltpu.VMEM(cells, BF16),
            pltpu.VMEM((WIDTH, WIDTH), BF16),
            pltpu.VMEM((LEVELS, 96, 2 * WIDTH), BF16),
            pltpu.VMEM((LEVELS, 64, 2 * WIDTH), BF16),
            pltpu.VMEM((2, LEVELS, 3, ROWS, WIDTH), BF16),
            pltpu.VMEM((LEVELS, 32, 2 * WIDTH), BF16),
            pltpu.VMEM((LEVELS, 96, 2 * WIDTH), F32),
            pltpu.VMEM((LEVELS, 32, 2 * WIDTH), F32),
            pltpu.VMEM((2, 2, 3, 2, 2, 2, HALF, 128), F32),
            pltpu.VMEM((HEADS, TOKENS, 128), F32),
            pltpu.VMEM((HEADS, TOKENS, 128), F32),
            pltpu.VMEM((HEADS, TOKENS, 128), F32),
            pltpu.VMEM((HEADS, TOKENS, 128), F32),
            pltpu.VMEM((4 * WIDTH, WIDTH), F32),
            pltpu.VMEM((1, WIDTH), F32),
            pltpu.VMEM((1024, 128), F32),
            pltpu.VMEM(cells, F32),
            pltpu.VMEM((LEVELS, 3, ROWS, WIDTH), BF16),
            pltpu.VMEM((LEVELS, 96, WIDTH), BF16),
            pltpu.VMEM((LEVELS, 3, ROWS, WIDTH), BF16),
            pltpu.VMEM((LEVELS, 64, WIDTH), BF16),
            pltpu.VMEM((LEVELS, 32, WIDTH), BF16),
            *per_chunk(LONS),
            *per_chunk(16),
            *per_chunk(8),
            *per_chunk(Z - 1),
            *per_chunk(LONS),
            pltpu.VMEM((48, 128), BF16),
            pltpu.VMEM((LATS, 48, 128), BF16),
            dma((8,)), dma((7,)), dma((7,)), dma((5, 4)), dma((5, 4)),
            dma((5, Z - 1)), dma((5, Z - 1)), dma((5, Z - 1)), dma((5, Z - 1)),
            dma((LATS - 1,)), dma((LATS - 1,)),
        ],
        compiler_params=pltpu.CompilerParams(
            vmem_limit_bytes=VMEM_LIMIT, collective_id=0, has_side_effects=True
        ),
        name="block",
    )(fields, out_grad, gain.reshape(1, WIDTH), qkv, out_weight, bias)


def hand_over_kernel(*refs):
    count = (len(refs) - 2) // 3
    sources, targets, held = refs[:count], refs[count : 2 * count], refs[2 * count : 3 * count]
    load_sem, store_sem = refs[-2:]
    loads, stores = [], []
    for k, (source, there, target) in enumerate(zip(sources, held, targets)):
        parts = [None]
        if source.shape[0] == 2 * 2 * HEADS * FLAT:
            parts = [pl.ds(part * 1296, 1296) for part in range(3)]
        elif len(source.shape) == 4:
            parts = [pl.ds(part * 2, 2) for part in range(2)]
        for p, part in enumerate(parts):
            a, b, c = (source, there, target) if part is None else (source.at[part], there.at[part], target.at[part])
            loads.append(pltpu.make_async_copy(a, b, load_sem.at[k, p]))
            stores.append(pltpu.make_async_copy(b, c, store_sem.at[k, p]))
    for c in loads:
        c.start()
    for a, b in zip(loads, stores):
        a.wait()
        b.start()
    for c in stores:
        c.wait()


def hand_over(arrays):
    hbm = pl.BlockSpec(memory_space=pl.ANY)
    dma = pltpu.SemaphoreType.DMA
    return pl.pallas_call(
        hand_over_kernel,
        out_shape=tuple(jax.ShapeDtypeStruct(a.shape, a.dtype) for a in arrays),
        in_specs=[hbm] * len(arrays),
        out_specs=(hbm,) * len(arrays),
        scratch_shapes=[pltpu.VMEM(a.shape, a.dtype) for a in arrays]
        + [dma((len(arrays), 3)), dma((len(arrays), 3))],
        compiler_params=pltpu.CompilerParams(vmem_limit_bytes=VMEM_LIMIT),
        name="hand_over",
    )(*arrays)


def local(fields, out_grad, gain, qkv_weight, out_weight, window_bias):
    tables = window_bias.transpose(0, 2, 1, 3).reshape(2, HEADS, 2, FLAT, 128)
    tables = with_layout_constraint(tables, Layout((0, 1, 3, 2, 4)))
    tables = tables.transpose(0, 1, 3, 2, 4).reshape(2 * 2 * HEADS * FLAT, 128)
    results = block(
        fields.transpose(0, 2, 1, 3), out_grad.transpose(0, 2, 1, 3), gain, qkv_weight, out_weight, tables
    )
    input_grad, qkv_grad, out_weight_grad, gain_grad, bias = hand_over(results)
    bias = bias.reshape(2, HEADS, FLAT, 2, 128).transpose(0, 1, 3, 2, 4)
    return (
        input_grad.transpose(0, 2, 1, 3),
        qkv_grad,
        out_weight_grad,
        gain_grad.reshape(WIDTH),
        bias.reshape(2, HEADS, 2, TOKENS * TOKENS).transpose(0, 2, 1, 3),
    )


def solution(mesh):
    in_specs = (
        P(None, "lat", "lon", None),
        P(None, "lat", "lon", None),
        P(),
        P(),
        P(),
        P("lat", None, None, None),
    )
    out_specs = (P(None, "lat", "lon", None), P(), P(), P(), P("lat", None, None, None))
    return jax.shard_map(local, mesh=mesh, in_specs=in_specs, out_specs=out_specs, check_vma=False)
```

```python
import jax
import jax.numpy as jnp
from jax import lax
from jax.experimental import pallas as pl
from jax.experimental.layout import Layout, with_layout_constraint
from jax.experimental.pallas import tpu as pltpu
from jax.sharding import PartitionSpec as P

F32 = jnp.float32
BF16 = jnp.bfloat16
MESH = pl.DeviceIdType.MESH

EPS = 1e-05
MASKED = -1e30
LOG2E = 1.4426950408889634

LEVELS = 4
ROWS = 24
COLS = 12
WIDTH = 192
HEADS = 6
HEAD = 32
TOKENS = 144
HALF = 72
FLAT = 162
LATS = 8
LONS = 32
Z = 8

CHUNK_ROWS = (32, 16, 32, 16, 48)
BIAS_CHUNKS = ((1, 0), (1, 1), (0, 0), (0, 1))
WEIGHTS = 4

VMEM_LIMIT = 56 * 1024 * 1024


def dot(a, b, contract=(1, 0)):
    return lax.dot_general(
        a, b, (((contract[0],), (contract[1],)), ((), ())), preferred_element_type=F32
    )


def remote(source, target, send, recv, there):
    return pltpu.make_async_remote_copy(
        src_ref=source, dst_ref=target, send_sem=send, recv_sem=recv, device_id=there, device_id_type=MESH
    )


def place_of(c):
    return c // 6, c % 6


def put_rows(win, at, start, rows):
    k, w, g, n, zl = at
    count = rows.shape[0]
    where_to = pl.ds(start, count, stride=6)
    win[k, w, g, n, 0, zl, where_to, :] = rows[:, :128]
    win[k, w, g, n, 1, zl, where_to, :] = jnp.concatenate([rows[:, 128:], jnp.zeros((count, 64), F32)], axis=1)


def take_rows(win, at, start, count):
    k, w, g, n, zl = at
    where_from = pl.ds(start, count, stride=6)
    return jnp.concatenate(
        [win[k, w, g, n, 0, zl, where_from, :], win[k, w, g, n, 1, zl, where_from, :][:, :64]], axis=1
    )


def take_window(win, at):
    return jnp.concatenate(
        [win[(*at, 0)].reshape(TOKENS, 128), win[(*at, 1)].reshape(TOKENS, 128)[:, :64]], axis=1
    )


def put_cells(own, win, k):
    @pl.loop(0, LEVELS)
    def _(z):
        lev, w, zl = (z + 1) % LEVELS, z // 2, z % 2
        for c in range(9):
            n, lo = place_of(c)
            tile = own[lev, c + 3].astype(F32)
            put_rows(win, (k, w, 0, n, zl), 36 + lo, tile[0:6])
            put_rows(win, (k, w, 1, n, zl), lo, tile[6:18])
            put_rows(win, (k, w, 2, 0, zl), 36 * n + lo, tile[18:24])


def put_east(east, win, k):
    @pl.loop(0, LEVELS)
    def _(z):
        lev, w, zl = (z + 1) % LEVELS, z // 2, z % 2
        for j in range(3):
            n, lo = place_of(9 + j)
            tile = east[k, lev, j].astype(F32)
            put_rows(win, (k, w, 0, n, zl), 36 + lo, tile[0:6])
            put_rows(win, (k, w, 1, n, zl), lo, tile[6:18])
            put_rows(win, (k, w, 2, 0, zl), 36 * n + lo, tile[18:24])


def put_above(above, corner, above32, corner32, win, lat):
    @pl.loop(0, LEVELS)
    def _(z):
        lev, w, zl = (z + 1) % LEVELS, z // 2, z % 2
        above32[lev, 0:64] = jnp.where(lat == 0, 0.0, above[lev].astype(F32))
        corner32[lev] = jnp.where(lat == 0, 0.0, corner[lev].astype(F32))
        for k in range(2):
            lanes = slice(k * WIDTH, (k + 1) * WIDTH)
            for c in range(12):
                n, lo = place_of(c)
                if c < 9:
                    cells = above32[lev, c * 6 : c * 6 + 6, lanes]
                else:
                    cells = corner32[lev, (c - 9) * 6 : (c - 9) * 6 + 6, lanes]
                put_rows(win, (k, w, 0, n, zl), lo, cells)


def window(win, w, g, n, gain, qkv_ref, query_t_ref, out_ref, masked, bias_acc, weight_acc, gain_acc):
    masked_lo, masked_hi = masked
    acc_lo, acc_hi = bias_acc
    scale = HEAD ** (-0.5)
    x = take_window(win, (0, w, g, n))
    centred = x - jnp.mean(x, axis=-1, keepdims=True)
    inv_std = lax.rsqrt(jnp.mean(centred * centred, axis=-1, keepdims=True) + EPS)
    standard = centred * inv_std
    normed = (standard * gain).astype(BF16)
    upstream32 = take_window(win, (1, w, g, n))
    upstream = upstream32.astype(BF16)
    projected = dot(normed, qkv_ref[...]).astype(BF16)
    queries_t = dot(query_t_ref[...], normed, (1, 1)).astype(BF16)
    attended_grad = dot(upstream, out_ref[...], (1, 1)).astype(BF16)
    attended_grad_t = dot(out_ref[...], upstream, (1, 1)).astype(BF16)
    lane = lax.broadcasted_iota(jnp.int32, (TOKENS, WIDTH), 1)
    own = [(lane // HEAD) == h for h in range(HEADS)]
    zero = jnp.zeros((), BF16)
    queries_all = jnp.concatenate([jnp.where(own[h], projected[:, :WIDTH], zero) for h in range(HEADS)], axis=0)
    upper_all = jnp.concatenate([jnp.where(own[h], attended_grad, zero) for h in range(HEADS)], axis=0)
    keys = projected[:, WIDTH : 2 * WIDTH]
    values = projected[:, 2 * WIDTH :]
    scores_all = dot(queries_all, keys, (1, 1))
    grads_all = dot(upper_all, values, (1, 1))
    keys_parts, values_parts, lows, scores_lows = [], [], [], []
    for h in range(HEADS):
        at = slice(h * TOKENS, (h + 1) * TOKENS)
        rows = slice(h * HEAD, (h + 1) * HEAD)
        table = jnp.concatenate([masked_lo[h], masked_hi[h, :, :16]], axis=1)
        scores = scores_all[at] * (scale * LOG2E) + table
        exps = jnp.exp2(scores - jnp.max(scores, axis=-1, keepdims=True))
        attention = exps * (1.0 / jnp.sum(exps, axis=-1, keepdims=True))
        low = attention.astype(BF16)
        attention_grad = grads_all[at]
        delta = jnp.sum(attention * attention_grad, axis=-1, keepdims=True)
        scores_grad = attention * (attention_grad - delta)
        acc_lo[h] += scores_grad[:, :128]
        acc_hi[h, :, :16] += scores_grad[:, 128:]
        scores_low = scores_grad.astype(BF16)
        lows.append(low)
        scores_lows.append(scores_low)
        values_parts.append(dot(attended_grad_t[rows], low).astype(BF16))
        keys_parts.append((dot(queries_t[rows], scores_low) * scale).astype(BF16))
    attended_all = dot(jnp.concatenate(lows, axis=0), values)
    queries_grad_all = dot(jnp.concatenate(scores_lows, axis=0), keys)
    attended_sum = jnp.zeros((TOKENS, WIDTH), F32)
    queries_sum = jnp.zeros((TOKENS, WIDTH), F32)
    for h in range(HEADS):
        at = slice(h * TOKENS, (h + 1) * TOKENS)
        attended_sum = jnp.where(own[h], attended_all[at], attended_sum)
        queries_sum = jnp.where(own[h], queries_grad_all[at], queries_sum)
    attended_t = jnp.transpose(attended_sum.astype(BF16))
    queries_grad_t = jnp.transpose((queries_sum * scale).astype(BF16))
    projected_grad_t = jnp.concatenate([queries_grad_t] + keys_parts + values_parts, axis=0)
    weight_acc[3 * WIDTH :, :] += dot(attended_t, upstream)
    weight_acc[: 3 * WIDTH, :] += dot(projected_grad_t, normed)
    shifted_t = dot(qkv_ref[...], projected_grad_t)
    grad = jnp.transpose(shifted_t.astype(BF16)).astype(F32)
    product = grad * standard
    gain_acc[...] += jnp.sum(product, axis=0, keepdims=True)
    scaled = grad * gain
    ig = upstream32 + inv_std * (
        scaled
        - jnp.mean(scaled, axis=-1, keepdims=True)
        - standard * jnp.mean(product * gain, axis=-1, keepdims=True)
    )
    win[0, w, g, n, 0] = ig[:, :128].reshape(2, HALF, 128)
    win[0, w, g, n, 1, :, :, 0:64] = ig[:, 128:].reshape(2, HALF, 64)


def mask_bias(masked, bias_ref, w, g, lat):
    masked_lo, masked_hi = masked
    table = jnp.minimum(g, 1)
    lane = lax.broadcasted_iota(jnp.int32, (18, 128), 1)

    def low(token):
        return (token // 6) % 12 < 6

    for i in range(8):
        q = 8 * lax.broadcasted_iota(jnp.int32, (18, 1), 0) + i

        def blocked(k):
            half = ((q >= HALF) != (k >= HALF)) & (w == 1)
            top = (low(q) | low(k)) & (g == 0) & (lat == 0)
            bottom = (low(q) != low(k)) & (g == 2)
            return half | top | bottom

        k = lax.broadcasted_iota(jnp.int32, (1, 128), 1)
        blocked_lo, blocked_hi = blocked(k), blocked(k + 128)
        for h in range(HEADS):
            at = (table * HEADS + h) * (2 * FLAT) + w + 2 * i
            first = bias_ref[pl.ds(at, 18, stride=18), :]
            second = bias_ref[pl.ds(at + 2, 18, stride=18), :]
            lo = jnp.where(lane >= 16 * i, first, second)
            hi = second
            if i:
                lo = pltpu.roll(lo, 128 - 16 * i, 1)
                hi = pltpu.roll(hi, 128 - 16 * i, 1)
            masked_lo[h, pl.ds(i, 18, stride=8), :] = jnp.where(blocked_lo, MASKED, lo * LOG2E)
            masked_hi[h, pl.ds(i, 18, stride=8), :] = jnp.where(blocked_hi, MASKED, hi * LOG2E)


def double_mask(masked):
    masked_lo, masked_hi = masked
    k = lax.broadcasted_iota(jnp.int32, (36, 128), 1)
    own = (k // 6) % 12 >= 6
    for h in range(HEADS):
        for at in (0, HALF):
            rows = pltpu.roll(masked_lo[h, at : at + 36, :], 36, 1)
            masked_lo[h, at + 36 : at + 72, :] = jnp.where(own, rows, MASKED)
            masked_hi[h, at + 36 : at + 72, :] = rows


def join_sums(bias_acc, own_acc):
    acc_lo, acc_hi = bias_acc
    own_lo, own_hi = own_acc
    lane = lax.broadcasted_iota(jnp.int32, (36, 128), 1)
    for h in range(HEADS):
        for at in (0, HALF):
            second = slice(at + 36, at + 72)
            lo, hi = pltpu.roll(own_lo[h, second, :], 92, 1), pltpu.roll(own_hi[h, second, :], 92, 1)
            acc_lo[h, at : at + 36, :] += own_lo[h, at : at + 36, :] + jnp.where(lane < 92, lo, hi)


def fold(w, bias_acc, flat, src):
    acc_lo, acc_hi = bias_acc
    groups = (18, 9)[w]
    lane = lax.broadcasted_iota(jnp.int32, (groups, 128), 1)

    def take(ref, h, i):
        value = ref[h, pl.ds(i, groups, stride=8), :]
        return value + ref[h, pl.ds(HALF + i, groups, stride=8), :] if w else value

    for h in range(HEADS):
        before_lo = before_hi = None
        for i in range(9):
            if i < 8:
                lo, hi = take(acc_lo, h, i), take(acc_hi, h, i)
                if i:
                    lo, hi = pltpu.roll(lo, 16 * i, 1), pltpu.roll(hi, 16 * i, 1)
            rows = lo
            if i:
                rows = jnp.where(lane >= 16 * (i - 1), before_hi, before_lo)
                if i < 8:
                    rows = jnp.where(lane >= 16 * i, lo, rows)
            flat[pl.ds(h * 9 * groups + i, groups, stride=9), :] = rows
            before_lo, before_hi = lo, hi
    each = (32, 16)[w]
    flat[HEADS * 9 * groups : LONS * each, :] = jnp.zeros((LONS * each - HEADS * 9 * groups, 128), F32)
    src[...] = flat[: LONS * each, :].astype(BF16).reshape(LONS, each, 128)


def fold_weights(weight_acc, gain_acc, src):
    for s in range(16):
        src[s] = weight_acc[s * 48 : (s + 1) * 48, :128].astype(BF16)
    for s in range(8):
        pair = jnp.concatenate(
            [weight_acc[s * 48 : (s + 1) * 48, 128:], weight_acc[384 + s * 48 : 384 + (s + 1) * 48, 128:]], axis=1
        )
        src[16 + s] = pair.astype(BF16)
    total = gain_acc[...]
    left = jnp.broadcast_to(total[:, :128], (48, 128))
    right = jnp.concatenate([total[:, 128:], jnp.zeros((1, 64), F32)], axis=1)
    right = jnp.broadcast_to(right, (48, 128))
    row = lax.broadcasted_iota(jnp.int32, (48, 128), 0)
    src[24] = jnp.where(row == 0, left, jnp.where(row == 1, right, 0.0)).astype(BF16)
    src[25:] = jnp.zeros((LONS - 25, 48, 128), BF16)


def unfold(g, w, out, flat, bias_out):
    each = (32, 16)[w]
    flat[: LONS * each, :] = out[...].reshape(LONS * each, 128).astype(F32)
    row = lax.broadcasted_iota(jnp.int32, (81, 128), 0)
    lane = lax.broadcasted_iota(jnp.int32, (81, 128), 1)
    left = (128 * row + lane) % TOKENS < HALF
    for h in range(HEADS):
        at = (g * HEADS + h) * (2 * FLAT) + w
        if w == 0:
            bias_out[pl.ds(at, FLAT, stride=2), :] = flat[h * FLAT : (h + 1) * FLAT, :]
        else:
            rows = flat[h * 81 : (h + 1) * 81, :]
            bias_out[pl.ds(at, 81, stride=2), :] = jnp.where(left, rows, 0.0)
            bias_out[pl.ds(at + FLAT, 81, stride=2), :] = jnp.where(left, 0.0, rows)


def unfold_weights(out, weight, qkv_ref, out_ref, gain_ref):
    for s in range(16):
        weight[s * 48 : (s + 1) * 48, :128] = out[s].astype(F32)
    for s in range(8):
        pair = out[16 + s].astype(F32)
        weight[s * 48 : (s + 1) * 48, 128:] = pair[:, :64]
        weight[384 + s * 48 : 384 + (s + 1) * 48, 128:] = pair[:, 64:]
    gain = out[24, 0:16, :].astype(F32)
    gain_ref[:, :128] = gain[0:1, :]
    gain_ref[:, 128:] = gain[1:2, :64]
    qkv_ref[...] = jnp.transpose(weight[: 3 * WIDTH, :])
    out_ref[...] = weight[3 * WIDTH :, :]


def kernel(
    fields_hbm, grad_hbm, gain_ref, qkv_ref, out_w_ref, bias_hbm,
    cells_out, qkv_grad_ref, out_grad_ref, gain_grad_ref, bias_out,
    fields, grads, bias, query_t,
    a_send, a_recv, b_recv, c_recv, pack32, corner32,
    win, masked_lo, masked_hi, acc_lo, acc_hi, own_lo, own_hi, weight_acc, gain_acc, flat,
    tiles, d_send, e_send, d_recv, e_recv, f_recv,
    src0, src1, src2, src3, src4, core0, core1, core2, core3, core4,
    xb0, xb1, xb2, xb3, xb4, zb0, zb1, zb2, zb3, zb4, out0, out1, out2, out3, out4,
    lat_send_buf, lat_buf,
    local_sem, halo_send, halo_recv, pair_send, pair_recv, z_send, z_recv, gz_send, gz_recv, lat_send, lat_recv,
):
    masked, bias_acc = (masked_lo, masked_hi), (acc_lo, acc_hi)
    lat = lax.axis_index("lat")
    lon = lax.axis_index("lon")
    last = lat == LATS - 1
    z, x, core = lon // 4, (lon // 2) % 2, lon % 2
    up, down = (lat + LATS - 1) % LATS, (lat + 1) % LATS
    west, east = (lon + LONS - 1) % LONS, (lon + 1) % LONS

    def at_lon(zz, xx, cc):
        return (lat, zz * 4 + xx * 2 + cc)

    core_peer = at_lon(z, x, 1 - core)
    x_peer = at_lon(z, 1 - x, core)
    z_peers = [at_lon((z + d) % Z, x, core) for d in range(1, Z)]
    lat_peers = [((lat + d) % LATS, lon) for d in range(1, LATS)]

    loads = [
        pltpu.make_async_copy(fields_hbm, fields, local_sem.at[0]),
        pltpu.make_async_copy(grad_hbm, grads, local_sem.at[1]),
        pltpu.make_async_copy(bias_hbm, bias, local_sem.at[2]),
    ]
    for c in loads:
        c.start()
    barrier = pltpu.get_barrier_semaphore()
    greeted = [core_peer, x_peer, (lat, west), (lat, east), (down, west), (up, east)] + z_peers + lat_peers
    for there in greeted:
        pl.semaphore_signal(barrier, inc=1, device_id=there, device_id_type=MESH)

    loads[0].wait()
    loads[1].wait()

    @pl.loop(0, LEVELS)
    def _(lev):
        for k, own in enumerate((fields, grads)):
            for col in range(COLS):
                at = (col - 3) * 6 if col >= 3 else 64 + col * 6
                pack32[lev, at : at + 6, k * WIDTH : (k + 1) * WIDTH] = own[lev, col].astype(F32)[18:24]
        a_send[lev] = pack32[lev].astype(BF16)

    pl.semaphore_wait(barrier, len(greeted))
    b_copies = [
        remote(own.at[:, 0:3], b_recv.at[k], halo_send.at[k], halo_recv.at[k], (lat, west))
        for k, own in enumerate((fields, grads))
    ]
    a_copy = remote(a_send.at[:, 0:64], a_recv, halo_send.at[2], halo_recv.at[2], (down, lon))
    c_copy = remote(a_send.at[:, 64:96], c_recv, halo_send.at[3], halo_recv.at[3], (down, west))
    for c in b_copies:
        c.start()

    @pl.when(lat < LATS - 1)
    def _():
        a_copy.start()
        c_copy.start()

    weight_acc[...] = jnp.zeros_like(weight_acc)
    gain_acc[...] = jnp.zeros_like(gain_acc)
    query_t[...] = jnp.transpose(qkv_ref[:, :WIDTH].astype(F32)).astype(BF16)
    for k, own in enumerate((fields, grads)):
        put_cells(own, win, k)
    loads[2].wait()
    srcs = (src0, src1, src2, src3, src4)
    core_bufs = (core0, core1, core2, core3, core4)
    x_bufs = (xb0, xb1, xb2, xb3, xb4)
    z_bufs = (zb0, zb1, zb2, zb3, zb4)
    outs = (out0, out1, out2, out3, out4)
    mine = core * 16 + x * 8 + z

    def core_copy(c):
        return remote(
            srcs[c].at[pl.ds((1 - core) * 16, 16)], core_bufs[c], pair_send.at[c, 0], pair_recv.at[c, 0], core_peer
        )

    def x_copy(c):
        return remote(
            srcs[c].at[pl.ds(core * 16 + (1 - x) * 8, 8)], x_bufs[c], pair_send.at[c, 1], pair_recv.at[c, 1], x_peer
        )

    def z_copies(c):
        return [
            remote(
                srcs[c].at[core * 16 + x * 8 + (z + d) % Z], z_bufs[c].at[d - 1],
                z_send.at[c, d - 1], z_recv.at[c, d - 1], z_peers[d - 1],
            )
            for d in range(1, Z)
        ]

    def gz_copies(c):
        part = outs[c].at[mine]
        return [remote(part, part, gz_send.at[c, d - 1], gz_recv.at[c, d - 1], z_peers[d - 1]) for d in range(1, Z)]

    def gx_copy(c):
        part = outs[c].at[pl.ds(core * 16 + x * 8, 8)]
        return remote(part, part, pair_send.at[c, 2], pair_recv.at[c, 2], x_peer)

    def gc_copy(c):
        part = outs[c].at[pl.ds(core * 16, 16)]
        return remote(part, part, pair_send.at[c, 3], pair_recv.at[c, 3], core_peer)

    lat_copies = [
        remote(lat_send_buf, lat_buf.at[lat], lat_send.at[d - 1], lat_recv.at[d - 1], lat_peers[d - 1])
        for d in range(1, LATS)
    ]

    def start(copies):
        for c in copies:
            c.start()

    def wait(copies):
        for c in copies:
            c.wait()

    def add_core(c):
        core_copy(c).wait()
        half = pl.ds(core * 16, 16)
        srcs[c][half] = (srcs[c][half].astype(F32) + core_bufs[c][...].astype(F32)).astype(BF16)
        x_copy(c).start()

    def add_x(c):
        x_copy(c).wait()
        part = pl.ds(core * 16 + x * 8, 8)
        srcs[c][part] = (srcs[c][part].astype(F32) + x_bufs[c][...].astype(F32)).astype(BF16)
        start(z_copies(c))

    def add_z(c):
        wait(z_copies(c))
        total = srcs[c][mine].astype(F32)
        for d in range(Z - 1):
            total = total + z_bufs[c][d].astype(F32)
        return total.astype(BF16)

    def gather_z(c):
        outs[c][mine] = add_z(c)
        start(gz_copies(c))

    def gather_x(c):
        wait(gz_copies(c))
        gx_copy(c).start()

    def gather_core(c):
        gx_copy(c).wait()
        gc_copy(c).start()

    def finish(c):
        gc_copy(c).wait()
        g, w = BIAS_CHUNKS[c]
        unfold(g, w, outs[c], flat, bias_out)

    @pl.loop(0, 6)
    def _(t):
        early = jnp.where(t < 4, 1, 0)
        g = early * (1 + t % 2)
        w = early * (t // 2) + (1 - early) * (t - 4)

        @pl.when(t == 4)
        def _():
            @pl.when(lat < LATS - 1)
            def _():
                a_copy.wait_send()
                c_copy.wait_send()

            @pl.when(lat > 0)
            def _():
                a_copy.wait_recv()
                c_copy.wait_recv()

            put_above(a_recv, c_recv, pack32, corner32, win, lat)

        @pl.when((t == 0) | (t == 2) | (t >= 4))
        def _():
            acc_lo[...] = jnp.zeros_like(acc_lo)
            acc_hi[...] = jnp.zeros_like(acc_hi)

        def run(n, acc):
            window(win, w, g, n, gain_ref[...], qkv_ref, query_t, out_w_ref, masked, acc, weight_acc, gain_acc)

        @pl.when((g == 2) & last)
        def _():
            mask_bias(masked, bias, w, g, lat)
            double_mask(masked)
            own_lo[...] = jnp.zeros_like(own_lo)
            own_hi[...] = jnp.zeros_like(own_hi)
            run(0, (own_lo, own_hi))
            join_sums(bias_acc, (own_lo, own_hi))

        @pl.when(g < 2)
        def _():
            mask_bias(masked, bias, w, g, lat)
            run(0, bias_acc)

            @pl.when(t == 0)
            def _():
                for c in b_copies:
                    c.wait()
                for k in range(2):
                    put_east(b_recv, win, k)

            run(1, bias_acc)

        @pl.when(t == 1)
        def _():
            fold(0, bias_acc, flat, src0)
            core_copy(0).start()

        @pl.when(t == 3)
        def _():
            fold(1, bias_acc, flat, src1)
            core_copy(1).start()
            add_core(0)

        @pl.when(t == 4)
        def _():
            fold(0, bias_acc, flat, src2)
            core_copy(2).start()
            add_core(1)
            add_x(0)

        @pl.when(t == 5)
        def _():
            fold_weights(weight_acc, gain_acc, src4)
            core_copy(4).start()
            fold(1, bias_acc, flat, src3)
            core_copy(3).start()
            add_core(2)
            add_x(1)
            gather_z(0)


    add_core(4)
    add_core(3)

    @pl.loop(0, LEVELS)
    def _(zz):
        lev, w, zl = (zz + 1) % LEVELS, zz // 2, zz % 2
        for c in range(COLS):
            n, lo = place_of(c)
            col = (c + 3) % COLS
            tiles[lev, col, 0:6, :] = take_rows(win, (0, w, 0, n, zl), 36 + lo, 6)
            tiles[lev, col, 6:18, :] = take_rows(win, (0, w, 1, n, zl), lo, 12)
            tiles[lev, col, 18:24, :] = take_rows(win, (0, w, 2, 0, zl), 36 * n + lo, 6)
            if c >= 9:
                d_send[lev, col] = tiles[lev, col].astype(BF16)
            at = c * 6 if c < 9 else 64 + (c - 9) * 6
            pack32[lev, at : at + 6, 0:WIDTH] = take_rows(win, (0, w, 0, n, zl), lo, 6)
        e_send[lev] = pack32[lev, :, 0:WIDTH].astype(BF16)

    d_copy = remote(d_send, d_recv, halo_send.at[4], halo_recv.at[4], (lat, east))
    e_copy = remote(e_send.at[:, 0:64], e_recv, halo_send.at[5], halo_recv.at[5], (up, lon))
    f_copy = remote(e_send.at[:, 64:96], f_recv, halo_send.at[6], halo_recv.at[6], (up, east))
    d_copy.start()

    @pl.when(lat > 0)
    def _():
        e_copy.start()
        f_copy.start()

    add_x(4)
    add_x(3)
    add_x(2)
    gather_z(1)
    gather_x(0)
    lat_send_buf[...] = add_z(4)
    lat_buf[lat] = lat_send_buf[...]
    start(lat_copies)
    gather_z(3)
    gather_z(2)
    gather_x(1)
    gather_core(0)
    d_copy.wait()

    @pl.when(lat > 0)
    def _():
        e_copy.wait_send()
        f_copy.wait_send()

    @pl.when(lat < LATS - 1)
    def _():
        e_copy.wait_recv()
        f_copy.wait_recv()

    @pl.loop(0, LEVELS)
    def _(lev):
        pack32[lev, 0:64, 0:WIDTH] = e_recv[lev].astype(F32)
        corner32[lev, :, 0:WIDTH] = f_recv[lev].astype(F32)
        for col in range(COLS):
            if col < 3:
                tiles[lev, col] = d_recv[lev, col].astype(F32)
                cells = corner32[lev, col * 6 : col * 6 + 6, 0:WIDTH]
            else:
                cells = pack32[lev, (col - 3) * 6 : (col - 3) * 6 + 6, 0:WIDTH]
            tiles[lev, col, 18:24, :] = jnp.where(last, tiles[lev, col, 18:24, :], cells)
            cells_out[lev, col] = tiles[lev, col].astype(BF16)

    finish(0)
    gather_x(3)
    gather_x(2)
    gather_core(1)
    wait(lat_copies)
    total = lat_buf[0].astype(F32)
    for i in range(1, LATS):
        total = total + lat_buf[i].astype(F32)
    outs[4][mine] = total.astype(BF16)
    start(gz_copies(4))
    finish(1)
    gather_core(3)
    gather_core(2)
    gather_x(4)
    finish(2)
    finish(3)
    gather_core(4)
    gc_copy(4).wait()
    unfold_weights(outs[4], weight_acc, qkv_grad_ref, out_grad_ref, gain_grad_ref)


def block(fields, out_grad, gain, qkv, out_weight, bias):
    dma = pltpu.SemaphoreType.DMA
    vmem = pl.BlockSpec(memory_space=pltpu.VMEM)
    hbm = pl.BlockSpec(memory_space=pl.ANY)

    def per_chunk(count):
        return [pltpu.VMEM((count, rows, 128), BF16) for rows in CHUNK_ROWS]

    cells = (LEVELS, COLS, ROWS, WIDTH)
    tables = (2 * 2 * HEADS * FLAT, 128)
    return pl.pallas_call(
        kernel,
        out_shape=(
            pltpu.VMEM(cells, BF16),
            pltpu.VMEM((WIDTH, 3 * WIDTH), F32),
            pltpu.VMEM((WIDTH, WIDTH), F32),
            pltpu.VMEM((1, WIDTH), F32),
            pltpu.VMEM(tables, F32),
        ),
        in_specs=[hbm, hbm, vmem, vmem, vmem, hbm],
        out_specs=(vmem,) * 5,
        scratch_shapes=[
            pltpu.VMEM(cells, BF16),
            pltpu.VMEM(cells, BF16),
            pltpu.VMEM(tables, F32),
            pltpu.VMEM((WIDTH, WIDTH), BF16),
            pltpu.VMEM((LEVELS, 96, 2 * WIDTH), BF16),
            pltpu.VMEM((LEVELS, 64, 2 * WIDTH), BF16),
            pltpu.VMEM((2, LEVELS, 3, ROWS, WIDTH), BF16),
            pltpu.VMEM((LEVELS, 32, 2 * WIDTH), BF16),
            pltpu.VMEM((LEVELS, 96, 2 * WIDTH), F32),
            pltpu.VMEM((LEVELS, 32, 2 * WIDTH), F32),
            pltpu.VMEM((2, 2, 3, 2, 2, 2, HALF, 128), F32),
            pltpu.VMEM((HEADS, TOKENS, 128), F32),
            pltpu.VMEM((HEADS, TOKENS, 128), F32),
            pltpu.VMEM((HEADS, TOKENS, 128), F32),
            pltpu.VMEM((HEADS, TOKENS, 128), F32),
            pltpu.VMEM((HEADS, TOKENS, 128), F32),
            pltpu.VMEM((HEADS, TOKENS, 128), F32),
            pltpu.VMEM((4 * WIDTH, WIDTH), F32),
            pltpu.VMEM((1, WIDTH), F32),
            pltpu.VMEM((1024, 128), F32),
            pltpu.VMEM(cells, F32),
            pltpu.VMEM((LEVELS, 3, ROWS, WIDTH), BF16),
            pltpu.VMEM((LEVELS, 96, WIDTH), BF16),
            pltpu.VMEM((LEVELS, 3, ROWS, WIDTH), BF16),
            pltpu.VMEM((LEVELS, 64, WIDTH), BF16),
            pltpu.VMEM((LEVELS, 32, WIDTH), BF16),
            *per_chunk(LONS),
            *per_chunk(16),
            *per_chunk(8),
            *per_chunk(Z - 1),
            *per_chunk(LONS),
            pltpu.VMEM((48, 128), BF16),
            pltpu.VMEM((LATS, 48, 128), BF16),
            dma((8,)), dma((7,)), dma((7,)), dma((5, 4)), dma((5, 4)),
            dma((5, Z - 1)), dma((5, Z - 1)), dma((5, Z - 1)), dma((5, Z - 1)),
            dma((LATS - 1,)), dma((LATS - 1,)),
        ],
        compiler_params=pltpu.CompilerParams(
            vmem_limit_bytes=VMEM_LIMIT, collective_id=0, has_side_effects=True
        ),
        name="block",
    )(fields, out_grad, gain.reshape(1, WIDTH), qkv, out_weight, bias)


def hand_over_kernel(*refs):
    count = (len(refs) - 1) // 2
    copies = [pltpu.make_async_copy(a, b, refs[-1].at[k]) for k, (a, b) in enumerate(zip(refs, refs[count:-1]))]
    for c in copies:
        c.start()
    for c in copies:
        c.wait()


def hand_over(arrays):
    return pl.pallas_call(
        hand_over_kernel,
        out_shape=tuple(jax.ShapeDtypeStruct(a.shape, a.dtype) for a in arrays),
        in_specs=[pl.BlockSpec(memory_space=pltpu.VMEM)] * len(arrays),
        out_specs=(pl.BlockSpec(memory_space=pl.ANY),) * len(arrays),
        scratch_shapes=[pltpu.SemaphoreType.DMA((len(arrays),))],
        compiler_params=pltpu.CompilerParams(vmem_limit_bytes=8 * 1024 * 1024),
        name="hand_over",
    )(*arrays)


def local(fields, out_grad, gain, qkv_weight, out_weight, window_bias):
    tables = window_bias.transpose(0, 2, 1, 3).reshape(2, HEADS, 2, FLAT, 128)
    tables = with_layout_constraint(tables, Layout((0, 1, 3, 2, 4)))
    tables = tables.transpose(0, 1, 3, 2, 4).reshape(2 * 2 * HEADS * FLAT, 128)
    results = block(
        fields.transpose(0, 2, 1, 3), out_grad.transpose(0, 2, 1, 3), gain, qkv_weight, out_weight, tables
    )
    input_grad, qkv_grad, out_weight_grad, gain_grad, bias = hand_over(results)
    bias = bias.reshape(2, HEADS, FLAT, 2, 128).transpose(0, 1, 3, 2, 4)
    return (
        input_grad.transpose(0, 2, 1, 3),
        qkv_grad,
        out_weight_grad,
        gain_grad.reshape(WIDTH),
        bias.reshape(2, HEADS, 2, TOKENS * TOKENS).transpose(0, 2, 1, 3),
    )


def solution(mesh):
    in_specs = (
        P(None, "lat", "lon", None),
        P(None, "lat", "lon", None),
        P(),
        P(),
        P(),
        P("lat", None, None, None),
    )
    out_specs = (P(None, "lat", "lon", None), P(), P(), P(), P("lat", None, None, None))
    return jax.shard_map(local, mesh=mesh, in_specs=in_specs, out_specs=out_specs, check_vma=False)
```

```python
import jax
import jax.numpy as jnp
from jax import lax
from jax.experimental import pallas as pl
from jax.experimental.layout import Layout, with_layout_constraint
from jax.experimental.pallas import tpu as pltpu
from jax.sharding import PartitionSpec as P

F32 = jnp.float32
BF16 = jnp.bfloat16
MESH = pl.DeviceIdType.MESH

EPS = 1e-05
MASKED = -1e30
LOG2E = 1.4426950408889634

LEVELS = 4
ROWS = 24
COLS = 12
WIDTH = 192
HEADS = 6
HEAD = 32
TOKENS = 144
HALF = 72
FLAT = 162
LATS = 8
LONS = 32
Z = 8

CHUNK_ROWS = (32, 16, 32, 16, 48)
BIAS_CHUNKS = ((1, 0), (1, 1), (0, 0), (0, 1))
WEIGHTS = 4

VMEM_LIMIT = 56 * 1024 * 1024


def dot(a, b, contract=(1, 0)):
    return lax.dot_general(
        a, b, (((contract[0],), (contract[1],)), ((), ())), preferred_element_type=F32
    )


def remote(source, target, send, recv, there):
    return pltpu.make_async_remote_copy(
        src_ref=source, dst_ref=target, send_sem=send, recv_sem=recv, device_id=there, device_id_type=MESH
    )


def place_of(c):
    return c // 6, c % 6


def put_rows(win, at, start, rows):
    k, w, g, n, zl = at
    count = rows.shape[0]
    where_to = pl.ds(start, count, stride=6)
    win[k, w, g, n, 0, zl, where_to, :] = rows[:, :128]
    win[k, w, g, n, 1, zl, where_to, :] = jnp.concatenate([rows[:, 128:], jnp.zeros((count, 64), F32)], axis=1)


def take_rows(win, at, start, count):
    k, w, g, n, zl = at
    where_from = pl.ds(start, count, stride=6)
    return jnp.concatenate(
        [win[k, w, g, n, 0, zl, where_from, :], win[k, w, g, n, 1, zl, where_from, :][:, :64]], axis=1
    )


def take_window(win, at):
    return jnp.concatenate(
        [win[(*at, 0)].reshape(TOKENS, 128), win[(*at, 1)].reshape(TOKENS, 128)[:, :64]], axis=1
    )


def put_cells(own, win, k):
    @pl.loop(0, LEVELS)
    def _(z):
        lev, w, zl = (z + 1) % LEVELS, z // 2, z % 2
        for c in range(9):
            n, lo = place_of(c)
            tile = own[lev, c + 3].astype(F32)
            put_rows(win, (k, w, 0, n, zl), 36 + lo, tile[0:6])
            put_rows(win, (k, w, 1, n, zl), lo, tile[6:18])
            put_rows(win, (k, w, 2, 0, zl), 36 * n + lo, tile[18:24])


def put_east(east, win, k):
    @pl.loop(0, LEVELS)
    def _(z):
        lev, w, zl = (z + 1) % LEVELS, z // 2, z % 2
        for j in range(3):
            n, lo = place_of(9 + j)
            tile = east[k, lev, j].astype(F32)
            put_rows(win, (k, w, 0, n, zl), 36 + lo, tile[0:6])
            put_rows(win, (k, w, 1, n, zl), lo, tile[6:18])
            put_rows(win, (k, w, 2, 0, zl), 36 * n + lo, tile[18:24])


def put_above(above, corner, above32, corner32, win, lat):
    @pl.loop(0, LEVELS)
    def _(z):
        lev, w, zl = (z + 1) % LEVELS, z // 2, z % 2
        above32[lev, 0:64] = jnp.where(lat == 0, 0.0, above[lev].astype(F32))
        corner32[lev] = jnp.where(lat == 0, 0.0, corner[lev].astype(F32))
        for k in range(2):
            lanes = slice(k * WIDTH, (k + 1) * WIDTH)
            for c in range(12):
                n, lo = place_of(c)
                if c < 9:
                    cells = above32[lev, c * 6 : c * 6 + 6, lanes]
                else:
                    cells = corner32[lev, (c - 9) * 6 : (c - 9) * 6 + 6, lanes]
                put_rows(win, (k, w, 0, n, zl), lo, cells)


def window(win, w, g, n, gain, qkv_ref, query_t_ref, out_ref, masked, bias_acc, weight_acc, gain_acc):
    masked_lo, masked_hi = masked
    acc_lo, acc_hi = bias_acc
    scale = HEAD ** (-0.5)
    x = take_window(win, (0, w, g, n))
    centred = x - jnp.mean(x, axis=-1, keepdims=True)
    inv_std = lax.rsqrt(jnp.mean(centred * centred, axis=-1, keepdims=True) + EPS)
    standard = centred * inv_std
    normed = (standard * gain).astype(BF16)
    upstream32 = take_window(win, (1, w, g, n))
    upstream = upstream32.astype(BF16)
    projected = dot(normed, qkv_ref[...]).astype(BF16)
    queries_t = dot(query_t_ref[...], normed, (1, 1)).astype(BF16)
    attended_grad = dot(upstream, out_ref[...], (1, 1)).astype(BF16)
    attended_grad_t = dot(out_ref[...], upstream, (1, 1)).astype(BF16)
    lane = lax.broadcasted_iota(jnp.int32, (TOKENS, WIDTH), 1)
    own = [(lane // HEAD) == h for h in range(HEADS)]
    zero = jnp.zeros((), BF16)
    queries_all = jnp.concatenate([jnp.where(own[h], projected[:, :WIDTH], zero) for h in range(HEADS)], axis=0)
    upper_all = jnp.concatenate([jnp.where(own[h], attended_grad, zero) for h in range(HEADS)], axis=0)
    keys = projected[:, WIDTH : 2 * WIDTH]
    values = projected[:, 2 * WIDTH :]
    scores_all = dot(queries_all, keys, (1, 1))
    grads_all = dot(upper_all, values, (1, 1))
    keys_parts, values_parts, lows, scores_lows = [], [], [], []
    for h in range(HEADS):
        at = slice(h * TOKENS, (h + 1) * TOKENS)
        rows = slice(h * HEAD, (h + 1) * HEAD)
        table = jnp.concatenate([masked_lo[h], masked_hi[h, :, :16]], axis=1)
        scores = scores_all[at] * (scale * LOG2E) + table
        exps = jnp.exp2(scores - jnp.max(scores, axis=-1, keepdims=True))
        attention = exps * (1.0 / jnp.sum(exps, axis=-1, keepdims=True))
        low = attention.astype(BF16)
        attention_grad = grads_all[at]
        delta = jnp.sum(attention * attention_grad, axis=-1, keepdims=True)
        scores_grad = attention * (attention_grad - delta)
        acc_lo[h] += scores_grad[:, :128]
        acc_hi[h, :, :16] += scores_grad[:, 128:]
        scores_low = scores_grad.astype(BF16)
        lows.append(low)
        scores_lows.append(scores_low)
        values_parts.append(dot(attended_grad_t[rows], low).astype(BF16))
        keys_parts.append((dot(queries_t[rows], scores_low) * scale).astype(BF16))
    attended_all = dot(jnp.concatenate(lows, axis=0), values)
    queries_grad_all = dot(jnp.concatenate(scores_lows, axis=0), keys)
    attended_sum = jnp.zeros((TOKENS, WIDTH), F32)
    queries_sum = jnp.zeros((TOKENS, WIDTH), F32)
    for h in range(HEADS):
        at = slice(h * TOKENS, (h + 1) * TOKENS)
        attended_sum = jnp.where(own[h], attended_all[at], attended_sum)
        queries_sum = jnp.where(own[h], queries_grad_all[at], queries_sum)
    attended_t = jnp.transpose(attended_sum.astype(BF16))
    queries_grad_t = jnp.transpose((queries_sum * scale).astype(BF16))
    projected_grad_t = jnp.concatenate([queries_grad_t] + keys_parts + values_parts, axis=0)
    weight_acc[3 * WIDTH :, :] += dot(attended_t, upstream)
    weight_acc[: 3 * WIDTH, :] += dot(projected_grad_t, normed)
    shifted_t = dot(qkv_ref[...], projected_grad_t)
    grad = jnp.transpose(shifted_t.astype(BF16)).astype(F32)
    product = grad * standard
    gain_acc[...] += jnp.sum(product, axis=0, keepdims=True)
    scaled = grad * gain
    ig = upstream32 + inv_std * (
        scaled
        - jnp.mean(scaled, axis=-1, keepdims=True)
        - standard * jnp.mean(product * gain, axis=-1, keepdims=True)
    )
    win[0, w, g, n, 0] = ig[:, :128].reshape(2, HALF, 128)
    win[0, w, g, n, 1, :, :, 0:64] = ig[:, 128:].reshape(2, HALF, 64)


def mask_bias(masked, bias_ref, w, g, lat):
    masked_lo, masked_hi = masked
    table = jnp.minimum(g, 1)
    lane = lax.broadcasted_iota(jnp.int32, (18, 128), 1)

    def low(token):
        return (token // 6) % 12 < 6

    for i in range(8):
        q = 8 * lax.broadcasted_iota(jnp.int32, (18, 1), 0) + i

        def blocked(k):
            half = ((q >= HALF) != (k >= HALF)) & (w == 1)
            top = (low(q) | low(k)) & (g == 0) & (lat == 0)
            bottom = (low(q) != low(k)) & (g == 2)
            return half | top | bottom

        k = lax.broadcasted_iota(jnp.int32, (1, 128), 1)
        blocked_lo, blocked_hi = blocked(k), blocked(k + 128)
        for h in range(HEADS):
            at = (table * HEADS + h) * (2 * FLAT) + w + 2 * i
            first = bias_ref[pl.ds(at, 18, stride=18), :]
            second = bias_ref[pl.ds(at + 2, 18, stride=18), :]
            lo = jnp.where(lane >= 16 * i, first, second)
            hi = second
            if i:
                lo = pltpu.roll(lo, 128 - 16 * i, 1)
                hi = pltpu.roll(hi, 128 - 16 * i, 1)
            masked_lo[h, pl.ds(i, 18, stride=8), :] = jnp.where(blocked_lo, MASKED, lo * LOG2E)
            masked_hi[h, pl.ds(i, 18, stride=8), :] = jnp.where(blocked_hi, MASKED, hi * LOG2E)


def double_mask(masked):
    masked_lo, masked_hi = masked
    k = lax.broadcasted_iota(jnp.int32, (36, 128), 1)
    own = (k // 6) % 12 >= 6
    for h in range(HEADS):
        for at in (0, HALF):
            rows = pltpu.roll(masked_lo[h, at : at + 36, :], 36, 1)
            masked_lo[h, at + 36 : at + 72, :] = jnp.where(own, rows, MASKED)
            masked_hi[h, at + 36 : at + 72, :] = rows


def join_sums(bias_acc, own_acc):
    acc_lo, acc_hi = bias_acc
    own_lo, own_hi = own_acc
    lane = lax.broadcasted_iota(jnp.int32, (36, 128), 1)
    for h in range(HEADS):
        for at in (0, HALF):
            second = slice(at + 36, at + 72)
            lo, hi = pltpu.roll(own_lo[h, second, :], 92, 1), pltpu.roll(own_hi[h, second, :], 92, 1)
            acc_lo[h, at : at + 36, :] += own_lo[h, at : at + 36, :] + jnp.where(lane < 92, lo, hi)


def fold(w, bias_acc, flat, src):
    acc_lo, acc_hi = bias_acc
    groups = (18, 9)[w]
    lane = lax.broadcasted_iota(jnp.int32, (groups, 128), 1)

    def take(ref, h, i):
        value = ref[h, pl.ds(i, groups, stride=8), :]
        return value + ref[h, pl.ds(HALF + i, groups, stride=8), :] if w else value

    for h in range(HEADS):
        before_lo = before_hi = None
        for i in range(9):
            if i < 8:
                lo, hi = take(acc_lo, h, i), take(acc_hi, h, i)
                if i:
                    lo, hi = pltpu.roll(lo, 16 * i, 1), pltpu.roll(hi, 16 * i, 1)
            rows = lo
            if i:
                rows = jnp.where(lane >= 16 * (i - 1), before_hi, before_lo)
                if i < 8:
                    rows = jnp.where(lane >= 16 * i, lo, rows)
            flat[pl.ds(h * 9 * groups + i, groups, stride=9), :] = rows
            before_lo, before_hi = lo, hi
    each = (32, 16)[w]
    flat[HEADS * 9 * groups : LONS * each, :] = jnp.zeros((LONS * each - HEADS * 9 * groups, 128), F32)
    src[...] = flat[: LONS * each, :].astype(BF16).reshape(LONS, each, 128)


def fold_weights(weight_acc, gain_acc, src):
    for s in range(16):
        src[s] = weight_acc[s * 48 : (s + 1) * 48, :128].astype(BF16)
    for s in range(8):
        pair = jnp.concatenate(
            [weight_acc[s * 48 : (s + 1) * 48, 128:], weight_acc[384 + s * 48 : 384 + (s + 1) * 48, 128:]], axis=1
        )
        src[16 + s] = pair.astype(BF16)
    total = gain_acc[...]
    left = jnp.broadcast_to(total[:, :128], (48, 128))
    right = jnp.concatenate([total[:, 128:], jnp.zeros((1, 64), F32)], axis=1)
    right = jnp.broadcast_to(right, (48, 128))
    row = lax.broadcasted_iota(jnp.int32, (48, 128), 0)
    src[24] = jnp.where(row == 0, left, jnp.where(row == 1, right, 0.0)).astype(BF16)
    src[25:] = jnp.zeros((LONS - 25, 48, 128), BF16)


def unfold(g, w, out, flat, bias_out):
    each = (32, 16)[w]
    flat[: LONS * each, :] = out[...].reshape(LONS * each, 128).astype(F32)
    row = lax.broadcasted_iota(jnp.int32, (81, 128), 0)
    lane = lax.broadcasted_iota(jnp.int32, (81, 128), 1)
    left = (128 * row + lane) % TOKENS < HALF
    for h in range(HEADS):
        at = (g * HEADS + h) * (2 * FLAT) + w
        if w == 0:
            bias_out[pl.ds(at, FLAT, stride=2), :] = flat[h * FLAT : (h + 1) * FLAT, :]
        else:
            rows = flat[h * 81 : (h + 1) * 81, :]
            bias_out[pl.ds(at, 81, stride=2), :] = jnp.where(left, rows, 0.0)
            bias_out[pl.ds(at + FLAT, 81, stride=2), :] = jnp.where(left, 0.0, rows)


def unfold_weights(out, weight, qkv_ref, out_ref, gain_ref):
    for s in range(16):
        weight[s * 48 : (s + 1) * 48, :128] = out[s].astype(F32)
    for s in range(8):
        pair = out[16 + s].astype(F32)
        weight[s * 48 : (s + 1) * 48, 128:] = pair[:, :64]
        weight[384 + s * 48 : 384 + (s + 1) * 48, 128:] = pair[:, 64:]
    gain = out[24, 0:16, :].astype(F32)
    gain_ref[:, :128] = gain[0:1, :]
    gain_ref[:, 128:] = gain[1:2, :64]
    qkv_ref[...] = jnp.transpose(weight[: 3 * WIDTH, :])
    out_ref[...] = weight[3 * WIDTH :, :]


def kernel(
    fields_hbm, grad_hbm, gain_ref, qkv_ref, out_w_ref, bias_hbm,
    cells_out, qkv_grad_ref, out_grad_ref, gain_grad_ref, bias_out,
    fields, grads, bias, query_t,
    a_send, a_recv, b_recv, c_recv, pack32, corner32,
    win, masked_lo, masked_hi, acc_lo, acc_hi, own_lo, own_hi, weight_acc, gain_acc, flat,
    tiles, d_send, e_send, d_recv, e_recv, f_recv,
    src0, src1, src2, src3, src4, core0, core1, core2, core3, core4,
    xb0, xb1, xb2, xb3, xb4, zb0, zb1, zb2, zb3, zb4, out0, out1, out2, out3, out4,
    lat_send_buf, lat_buf,
    local_sem, halo_send, halo_recv, pair_send, pair_recv, z_send, z_recv, gz_send, gz_recv, lat_send, lat_recv,
):
    masked, bias_acc = (masked_lo, masked_hi), (acc_lo, acc_hi)
    lat = lax.axis_index("lat")
    lon = lax.axis_index("lon")
    last = lat == LATS - 1
    z, x, core = lon // 4, (lon // 2) % 2, lon % 2
    up, down = (lat + LATS - 1) % LATS, (lat + 1) % LATS
    west, east = (lon + LONS - 1) % LONS, (lon + 1) % LONS

    def at_lon(zz, xx, cc):
        return (lat, zz * 4 + xx * 2 + cc)

    core_peer = at_lon(z, x, 1 - core)
    x_peer = at_lon(z, 1 - x, core)
    z_peers = [at_lon((z + d) % Z, x, core) for d in range(1, Z)]
    lat_peers = [((lat + d) % LATS, lon) for d in range(1, LATS)]

    loads = [
        pltpu.make_async_copy(fields_hbm, fields, local_sem.at[0]),
        pltpu.make_async_copy(grad_hbm, grads, local_sem.at[1]),
        pltpu.make_async_copy(bias_hbm, bias.at[pl.ds(0, 2 * 2 * HEADS * FLAT)], local_sem.at[2]),
    ]
    for c in loads:
        c.start()
    barrier = pltpu.get_barrier_semaphore()
    greeted = [core_peer, x_peer, (lat, west), (lat, east), (down, west), (up, east)] + z_peers + lat_peers
    for there in greeted:
        pl.semaphore_signal(barrier, inc=1, device_id=there, device_id_type=MESH)

    loads[0].wait()
    loads[1].wait()

    @pl.loop(0, LEVELS)
    def _(lev):
        for k, own in enumerate((fields, grads)):
            for col in range(COLS):
                at = (col - 3) * 6 if col >= 3 else 64 + col * 6
                pack32[lev, at : at + 6, k * WIDTH : (k + 1) * WIDTH] = own[lev, col].astype(F32)[18:24]
        a_send[lev] = pack32[lev].astype(BF16)

    pl.semaphore_wait(barrier, len(greeted))
    b_copies = [
        remote(own.at[:, 0:3], b_recv.at[k], halo_send.at[k], halo_recv.at[k], (lat, west))
        for k, own in enumerate((fields, grads))
    ]
    a_copy = remote(a_send.at[:, 0:64], a_recv, halo_send.at[2], halo_recv.at[2], (down, lon))
    c_copy = remote(a_send.at[:, 64:96], c_recv, halo_send.at[3], halo_recv.at[3], (down, west))
    for c in b_copies:
        c.start()

    @pl.when(lat < LATS - 1)
    def _():
        a_copy.start()
        c_copy.start()

    weight_acc[...] = jnp.zeros_like(weight_acc)
    gain_acc[...] = jnp.zeros_like(gain_acc)
    query_t[...] = jnp.transpose(qkv_ref[:, :WIDTH].astype(F32)).astype(BF16)
    for k, own in enumerate((fields, grads)):
        put_cells(own, win, k)
    loads[2].wait()
    srcs = (src0, src1, src2, src3, src4)
    core_bufs = (core0, core1, core2, core3, core4)
    x_bufs = (xb0, xb1, xb2, xb3, xb4)
    z_bufs = (zb0, zb1, zb2, zb3, zb4)
    outs = (out0, out1, out2, out3, out4)
    mine = core * 16 + x * 8 + z

    def core_copy(c):
        return remote(
            srcs[c].at[pl.ds((1 - core) * 16, 16)], core_bufs[c], pair_send.at[c, 0], pair_recv.at[c, 0], core_peer
        )

    def x_copy(c):
        return remote(
            srcs[c].at[pl.ds(core * 16 + (1 - x) * 8, 8)], x_bufs[c], pair_send.at[c, 1], pair_recv.at[c, 1], x_peer
        )

    def z_copies(c):
        return [
            remote(
                srcs[c].at[core * 16 + x * 8 + (z + d) % Z], z_bufs[c].at[d - 1],
                z_send.at[c, d - 1], z_recv.at[c, d - 1], z_peers[d - 1],
            )
            for d in range(1, Z)
        ]

    def gz_copies(c):
        part = outs[c].at[mine]
        return [remote(part, part, gz_send.at[c, d - 1], gz_recv.at[c, d - 1], z_peers[d - 1]) for d in range(1, Z)]

    def gx_copy(c):
        part = outs[c].at[pl.ds(core * 16 + x * 8, 8)]
        return remote(part, part, pair_send.at[c, 2], pair_recv.at[c, 2], x_peer)

    def gc_copy(c):
        part = outs[c].at[pl.ds(core * 16, 16)]
        return remote(part, part, pair_send.at[c, 3], pair_recv.at[c, 3], core_peer)

    lat_copies = [
        remote(lat_send_buf, lat_buf.at[lat], lat_send.at[d - 1], lat_recv.at[d - 1], lat_peers[d - 1])
        for d in range(1, LATS)
    ]

    def start(copies):
        for c in copies:
            c.start()

    def wait(copies):
        for c in copies:
            c.wait()

    def add_core(c):
        core_copy(c).wait()
        half = pl.ds(core * 16, 16)
        srcs[c][half] = (srcs[c][half].astype(F32) + core_bufs[c][...].astype(F32)).astype(BF16)
        x_copy(c).start()

    def add_x(c):
        x_copy(c).wait()
        part = pl.ds(core * 16 + x * 8, 8)
        srcs[c][part] = (srcs[c][part].astype(F32) + x_bufs[c][...].astype(F32)).astype(BF16)
        start(z_copies(c))

    def add_z(c):
        wait(z_copies(c))
        total = srcs[c][mine].astype(F32)
        for d in range(Z - 1):
            total = total + z_bufs[c][d].astype(F32)
        return total.astype(BF16)

    def gather_z(c):
        outs[c][mine] = add_z(c)
        start(gz_copies(c))

    def gather_x(c):
        wait(gz_copies(c))
        gx_copy(c).start()

    def gather_core(c):
        gx_copy(c).wait()
        gc_copy(c).start()

    def finish(c):
        gc_copy(c).wait()
        g, w = BIAS_CHUNKS[c]
        unfold(g, w, outs[c], flat, bias_out)

    @pl.loop(0, 6)
    def _(t):
        early = jnp.where(t < 4, 1, 0)
        g = early * (1 + t % 2)
        w = early * (t // 2) + (1 - early) * (t - 4)

        @pl.when(t == 4)
        def _():
            @pl.when(lat < LATS - 1)
            def _():
                a_copy.wait_send()
                c_copy.wait_send()

            @pl.when(lat > 0)
            def _():
                a_copy.wait_recv()
                c_copy.wait_recv()

            put_above(a_recv, c_recv, pack32, corner32, win, lat)

        @pl.when((t == 0) | (t == 2) | (t >= 4))
        def _():
            acc_lo[...] = jnp.zeros_like(acc_lo)
            acc_hi[...] = jnp.zeros_like(acc_hi)

        def run(n, acc):
            window(win, w, g, n, gain_ref[...], qkv_ref, query_t, out_w_ref, masked, acc, weight_acc, gain_acc)

        @pl.when((g == 2) & last)
        def _():
            mask_bias(masked, bias, w, g, lat)
            double_mask(masked)
            own_lo[...] = jnp.zeros_like(own_lo)
            own_hi[...] = jnp.zeros_like(own_hi)
            run(0, (own_lo, own_hi))
            join_sums(bias_acc, (own_lo, own_hi))

        @pl.when(g < 2)
        def _():
            mask_bias(masked, bias, w, g, lat)
            run(0, bias_acc)

            @pl.when(t == 0)
            def _():
                for c in b_copies:
                    c.wait()
                for k in range(2):
                    put_east(b_recv, win, k)

            run(1, bias_acc)

        @pl.when(t == 1)
        def _():
            fold(0, bias_acc, flat, src0)
            core_copy(0).start()

        @pl.when(t == 3)
        def _():
            fold(1, bias_acc, flat, src1)
            core_copy(1).start()
            add_core(0)

        @pl.when(t == 4)
        def _():
            fold(0, bias_acc, flat, src2)
            core_copy(2).start()
            add_core(1)
            add_x(0)

        @pl.when(t == 5)
        def _():
            fold_weights(weight_acc, gain_acc, src4)
            core_copy(4).start()
            fold(1, bias_acc, flat, src3)
            core_copy(3).start()
            add_core(2)
            add_x(1)
            gather_z(0)


    add_core(4)
    add_core(3)

    @pl.loop(0, LEVELS)
    def _(zz):
        lev, w, zl = (zz + 1) % LEVELS, zz // 2, zz % 2
        for c in range(COLS):
            n, lo = place_of(c)
            col = (c + 3) % COLS
            tiles[lev, col, 0:6, :] = take_rows(win, (0, w, 0, n, zl), 36 + lo, 6)
            tiles[lev, col, 6:18, :] = take_rows(win, (0, w, 1, n, zl), lo, 12)
            tiles[lev, col, 18:24, :] = take_rows(win, (0, w, 2, 0, zl), 36 * n + lo, 6)
            if c >= 9:
                d_send[lev, col] = tiles[lev, col].astype(BF16)
            at = c * 6 if c < 9 else 64 + (c - 9) * 6
            pack32[lev, at : at + 6, 0:WIDTH] = take_rows(win, (0, w, 0, n, zl), lo, 6)
        e_send[lev] = pack32[lev, :, 0:WIDTH].astype(BF16)

    d_copy = remote(d_send, d_recv, halo_send.at[4], halo_recv.at[4], (lat, east))
    e_copy = remote(e_send.at[:, 0:64], e_recv, halo_send.at[5], halo_recv.at[5], (up, lon))
    f_copy = remote(e_send.at[:, 64:96], f_recv, halo_send.at[6], halo_recv.at[6], (up, east))
    d_copy.start()

    @pl.when(lat > 0)
    def _():
        e_copy.start()
        f_copy.start()

    add_x(4)
    add_x(3)
    add_x(2)
    gather_z(1)
    gather_x(0)
    lat_send_buf[...] = add_z(4)
    lat_buf[lat] = lat_send_buf[...]
    start(lat_copies)
    gather_z(3)
    gather_z(2)
    gather_x(1)
    gather_core(0)
    d_copy.wait()

    @pl.when(lat > 0)
    def _():
        e_copy.wait_send()
        f_copy.wait_send()

    @pl.when(lat < LATS - 1)
    def _():
        e_copy.wait_recv()
        f_copy.wait_recv()

    @pl.loop(0, LEVELS)
    def _(lev):
        pack32[lev, 0:64, 0:WIDTH] = e_recv[lev].astype(F32)
        corner32[lev, :, 0:WIDTH] = f_recv[lev].astype(F32)
        for col in range(COLS):
            if col < 3:
                tiles[lev, col] = d_recv[lev, col].astype(F32)
                cells = corner32[lev, col * 6 : col * 6 + 6, 0:WIDTH]
            else:
                cells = pack32[lev, (col - 3) * 6 : (col - 3) * 6 + 6, 0:WIDTH]
            tiles[lev, col, 18:24, :] = jnp.where(last, tiles[lev, col, 18:24, :], cells)
            cells_out[lev, col] = tiles[lev, col].astype(BF16)

    finish(0)
    gather_x(3)
    gather_x(2)
    gather_core(1)
    wait(lat_copies)
    total = lat_buf[0].astype(F32)
    for i in range(1, LATS):
        total = total + lat_buf[i].astype(F32)
    outs[4][mine] = total.astype(BF16)
    start(gz_copies(4))
    finish(1)
    gather_core(3)
    gather_core(2)
    gather_x(4)
    finish(2)
    finish(3)
    gather_core(4)
    gc_copy(4).wait()
    unfold_weights(outs[4], weight_acc, qkv_grad_ref, out_grad_ref, gain_grad_ref)


def block(fields, out_grad, gain, qkv, out_weight, bias):
    dma = pltpu.SemaphoreType.DMA
    vmem = pl.BlockSpec(memory_space=pltpu.VMEM)
    hbm = pl.BlockSpec(memory_space=pl.ANY)

    def per_chunk(count):
        return [pltpu.VMEM((count, rows, 128), BF16) for rows in CHUNK_ROWS]

    cells = (LEVELS, COLS, ROWS, WIDTH)
    padded = (2 * 2 * HEADS * FLAT + 144, 128)
    return pl.pallas_call(
        kernel,
        out_shape=(
            pltpu.VMEM(cells, BF16),
            pltpu.VMEM((WIDTH, 3 * WIDTH), F32),
            pltpu.VMEM((WIDTH, WIDTH), F32),
            pltpu.VMEM((1, WIDTH), F32),
            pltpu.VMEM(padded, F32),
        ),
        in_specs=[hbm, hbm, vmem, vmem, vmem, hbm],
        out_specs=(vmem,) * 5,
        scratch_shapes=[
            pltpu.VMEM(cells, BF16),
            pltpu.VMEM(cells, BF16),
            pltpu.VMEM(padded, F32),
            pltpu.VMEM((WIDTH, WIDTH), BF16),
            pltpu.VMEM((LEVELS, 96, 2 * WIDTH), BF16),
            pltpu.VMEM((LEVELS, 64, 2 * WIDTH), BF16),
            pltpu.VMEM((2, LEVELS, 3, ROWS, WIDTH), BF16),
            pltpu.VMEM((LEVELS, 32, 2 * WIDTH), BF16),
            pltpu.VMEM((LEVELS, 96, 2 * WIDTH), F32),
            pltpu.VMEM((LEVELS, 32, 2 * WIDTH), F32),
            pltpu.VMEM((2, 2, 3, 2, 2, 2, HALF, 128), F32),
            pltpu.VMEM((HEADS + 1, TOKENS, 128), F32),
            pltpu.VMEM((HEADS + 1, TOKENS, 128), F32),
            pltpu.VMEM((HEADS + 1, TOKENS, 128), F32),
            pltpu.VMEM((HEADS + 1, TOKENS, 128), F32),
            pltpu.VMEM((HEADS + 1, TOKENS, 128), F32),
            pltpu.VMEM((HEADS + 1, TOKENS, 128), F32),
            pltpu.VMEM((4 * WIDTH, WIDTH), F32),
            pltpu.VMEM((1, WIDTH), F32),
            pltpu.VMEM((1152, 128), F32),
            pltpu.VMEM(cells, F32),
            pltpu.VMEM((LEVELS, 3, ROWS, WIDTH), BF16),
            pltpu.VMEM((LEVELS, 96, WIDTH), BF16),
            pltpu.VMEM((LEVELS, 3, ROWS, WIDTH), BF16),
            pltpu.VMEM((LEVELS, 64, WIDTH), BF16),
            pltpu.VMEM((LEVELS, 32, WIDTH), BF16),
            *per_chunk(LONS),
            *per_chunk(16),
            *per_chunk(8),
            *per_chunk(Z - 1),
            *per_chunk(LONS),
            pltpu.VMEM((48, 128), BF16),
            pltpu.VMEM((LATS, 48, 128), BF16),
            dma((8,)), dma((7,)), dma((7,)), dma((5, 4)), dma((5, 4)),
            dma((5, Z - 1)), dma((5, Z - 1)), dma((5, Z - 1)), dma((5, Z - 1)),
            dma((LATS - 1,)), dma((LATS - 1,)),
        ],
        compiler_params=pltpu.CompilerParams(
            vmem_limit_bytes=VMEM_LIMIT, collective_id=0, has_side_effects=True
        ),
        name="block",
    )(fields, out_grad, gain.reshape(1, WIDTH), qkv, out_weight, bias)


def hand_over_kernel(*refs):
    count = (len(refs) - 1) // 2
    copies = [
        pltpu.make_async_copy(a.at[pl.ds(0, b.shape[0])], b, refs[-1].at[k])
        for k, (a, b) in enumerate(zip(refs, refs[count:-1]))
    ]
    for c in copies:
        c.start()
    for c in copies:
        c.wait()


def hand_over(arrays):
    return pl.pallas_call(
        hand_over_kernel,
        out_shape=tuple(
            jax.ShapeDtypeStruct((min(a.shape[0], 2 * 2 * HEADS * FLAT), *a.shape[1:]), a.dtype) for a in arrays
        ),
        in_specs=[pl.BlockSpec(memory_space=pltpu.VMEM)] * len(arrays),
        out_specs=(pl.BlockSpec(memory_space=pl.ANY),) * len(arrays),
        scratch_shapes=[pltpu.SemaphoreType.DMA((len(arrays),))],
        compiler_params=pltpu.CompilerParams(vmem_limit_bytes=8 * 1024 * 1024),
        name="hand_over",
    )(*arrays)


def local(fields, out_grad, gain, qkv_weight, out_weight, window_bias):
    tables = window_bias.transpose(0, 2, 1, 3).reshape(2, HEADS, 2, FLAT, 128)
    tables = with_layout_constraint(tables, Layout((0, 1, 3, 2, 4)))
    tables = tables.transpose(0, 1, 3, 2, 4).reshape(2 * 2 * HEADS * FLAT, 128)
    results = block(
        fields.transpose(0, 2, 1, 3), out_grad.transpose(0, 2, 1, 3), gain, qkv_weight, out_weight, tables
    )
    input_grad, qkv_grad, out_weight_grad, gain_grad, bias = hand_over(results)
    bias = bias.reshape(2, HEADS, FLAT, 2, 128).transpose(0, 1, 3, 2, 4)
    return (
        input_grad.transpose(0, 2, 1, 3),
        qkv_grad,
        out_weight_grad,
        gain_grad.reshape(WIDTH),
        bias.reshape(2, HEADS, 2, TOKENS * TOKENS).transpose(0, 2, 1, 3),
    )


def solution(mesh):
    in_specs = (
        P(None, "lat", "lon", None),
        P(None, "lat", "lon", None),
        P(),
        P(),
        P(),
        P("lat", None, None, None),
    )
    out_specs = (P(None, "lat", "lon", None), P(), P(), P(), P("lat", None, None, None))
    return jax.shard_map(local, mesh=mesh, in_specs=in_specs, out_specs=out_specs, check_vma=False)
```
